32 devices in a mesh: groups: 2 (over y), slab: 16 (over z, x, core).
Axes of the slice: x: 2, y: 2, z: 4, core: 2. Of those that a mesh axis runs over, the one named last changes fastest.
Arguments:
- estimate: float32 [128, 2048, 128], P('slab', 'groups'), parts along dimension 1, may hold values from 0.2 to 5
- recorded: float32 [4, 128, 2048, 128], P(None, 'slab', 'groups'), parts along dimension 2, may hold values from 0.2 to 5
- lateral: float32 [4, 2, 31], replicated, may hold values from 0.05 to 1
- axial_taps: float32 [4, 101], replicated, may hold values from 0.05 to 1
Outputs:
- restored: float32 [128, 2048, 128], P('slab', 'groups'), parts along dimension 1
The draws below stay inside these ranges and needn't reach their ends.
There are 2 independent parts, one for each index of `groups`. The reference program is written for one: setup_inputs(seed, part) draws one part's arguments, and reference() takes and returns one part's arrays. A program takes and returns all parts, laid end to end along the dimension named above; an argument that names none is the same for every part. Nothing has to cross between parts.
All inputs are finite; a program needn't handle non-finite values.
Results may differ from the reference program's by a relative error of at most 0.0001.
Values sent between devices are 32-bit elements; how exact they have to be, the bound alone decides.
No kernel may reach another device: no remote copies, remote signals or barrier semaphores. Data moves between devices by JAX's collectives and lax.ppermute only.
A program may use at most 192 MiB of HBM per device.

```python
import math
import jax
import jax.numpy as jnp
from jax import lax

X = 1024
Y = 128
Z = 128
KXY = 31
KZ = 101
VIEWS = 4


def shard_levels(key, shape, cuts, low, largest):
    def one(dim, shards_of):
        heights = jax.random.uniform(jax.random.fold_in(jax.random.fold_in(key, 6), dim), (shards_of,), jnp.float32, low / len(cuts), largest / len(cuts))
        return jnp.repeat(jnp.exp(heights), shape[dim] // shards_of).reshape((-1,) + (1,) * (len(shape) - dim - 1))

    gain = one(*cuts[0])
    for cut in cuts[1:]:
        gain = gain * one(*cut)
    return gain


def setup_inputs(seed: int = 0, part: int = 0) -> dict:
    key_list = jax.random.split(jax.random.key(seed), 5)
    part_splits = jax.random.split(jax.random.fold_in(key_list[4], part), 5)
    estimate = jnp.clip(jnp.exp(math.log(5.0) - 3.218876 * jax.random.uniform(part_splits[0], (Z, X, Y), jnp.float32) ** shard_levels(part_splits[0], (Z, X, Y), ((0, 16),), -0.2, 0.2)), 0.2, 5.0)
    recorded = jnp.clip(jnp.exp(math.log(5.0) - 3.218876 * jax.random.uniform(part_splits[1], (VIEWS, Z, X, Y), jnp.float32) ** shard_levels(part_splits[1], (VIEWS, Z, X, Y), ((1, 16),), -0.2, 0.2)), 0.2, 5.0)
    lateral = jnp.clip(jnp.exp(jax.random.uniform(key_list[2], (VIEWS, 2, KXY), jnp.float32, math.log(0.05), math.log(1.0))), 0.05, 1.0)
    axial_taps = jnp.clip(jnp.exp(jax.random.uniform(key_list[3], (VIEWS, KZ), jnp.float32, math.log(0.05), math.log(1.0))), 0.05, 1.0)
    return {"estimate": estimate, "recorded": recorded, "lateral": lateral, "axial_taps": axial_taps}


def correlate(volume, kernel, along):
    length = kernel.shape[0]
    margin = length // 2
    extent = volume.shape[along]
    widths = [(0, 0)] * volume.ndim
    widths[along] = (margin, margin)
    padded = jnp.pad(volume, widths)

    def accumulate(position, total):
        return total + kernel[position] * lax.dynamic_slice_in_dim(padded, position, extent, along)

    return lax.fori_loop(0, length, accumulate, jnp.zeros(volume.shape, jnp.float32))


def banded(kernel, extent):
    length = kernel.shape[0]
    margin = length // 2
    places = jnp.arange(extent, dtype=jnp.int32)
    offsets = places[None, :] - places[:, None] + margin
    stencil = jnp.arange(length, dtype=jnp.int32)
    picked = (offsets[None, :, :] == stencil[:, None, None]).astype(jnp.float32)
    return jnp.sum(kernel[:, None, None] * picked, axis=0)


def normalized(kernel):
    return kernel / jnp.sum(kernel)


def reference(estimate, recorded, lateral, axial_taps):
    current = estimate
    for which_view in range(VIEWS):
        row_taps = normalized(lateral[which_view, 0])
        column_taps = normalized(lateral[which_view, 1])
        depth_taps = normalized(axial_taps[which_view])
        matrix = banded(depth_taps, current.shape[0])
        blurred = correlate(correlate(current, row_taps[::-1], 1), column_taps[::-1], 2)
        blurred = jnp.tensordot(matrix.T, blurred, axes=(1, 0), precision=lax.Precision.HIGHEST)
        quotient = recorded[which_view] / blurred
        spread = jnp.tensordot(matrix, quotient, axes=(1, 0), precision=lax.Precision.HIGHEST)
        spread = correlate(correlate(spread, column_taps, 2), row_taps, 1)
        current = current * spread
    return current
```

```python
import functools

import jax
import jax.numpy as jnp
from jax import lax
from jax.experimental import pallas as pl
from jax.experimental.pallas import tpu as pltpu
from jax.sharding import PartitionSpec as P

VMEM_LIMIT = 56 * 1024 * 1024
WHOLE = pl.BlockSpec(memory_space=pltpu.VMEM)
SCALARS = pl.BlockSpec(memory_space=pltpu.SMEM)


def banded(kernel, extent):
    length = kernel.shape[0]
    margin = length // 2
    places = jnp.arange(extent, dtype=jnp.int32)
    offsets = places[None, :] - places[:, None] + margin
    stencil = jnp.arange(length, dtype=jnp.int32)
    picked = (offsets[None, :, :] == stencil[:, None, None]).astype(jnp.float32)
    return jnp.sum(kernel[:, None, None] * picked, axis=0)


def normalized(kernel):
    return kernel / jnp.sum(kernel)


def halves(value):
    high = value.astype(jnp.bfloat16)
    low = (value - high.astype(jnp.float32)).astype(jnp.bfloat16)
    return high, low


def position(device, run):
    row, place = device // run, device % run
    return row * run + jnp.where(row % 2 == 0, place, run - 1 - place)


def device_order(count, run):
    return [r * run + (p if r % 2 == 0 else run - 1 - p) for r in range(count // run) for p in range(run)]


def along_yz(load, store, matrix_y, matrix_z, rows):
    depth, width = matrix_z.shape[0], matrix_y.shape[0]
    right_high, right_low = halves(matrix_y)
    right = jnp.concatenate([right_high, right_low], axis=1)
    right = jnp.concatenate([right, right], axis=0)
    left_high, left_low = halves(matrix_z)
    left = jnp.concatenate([left_high, left_low], axis=0)
    left = jnp.concatenate([left, left], axis=1)

    def pair(index, _):
        row = 2 * index
        planes = jnp.concatenate([load(row), load(row + 1)], axis=0)
        product = jnp.dot(
            jnp.concatenate(halves(planes), axis=1), right, preferred_element_type=jnp.float32
        )
        mixed = product[:, :width] + product[:, width:]
        sides = jnp.concatenate([mixed[:depth], mixed[depth:]], axis=1)
        product = jnp.dot(
            left, jnp.concatenate(halves(sides), axis=0), preferred_element_type=jnp.float32
        )
        mixed = product[:depth] + product[depth:]
        store(row, mixed[:, :width])
        store(row + 1, mixed[:, width:])
        return 0

    lax.fori_loop(0, rows // 2, pair, 0, unroll=4)


def along_x(center, above, below, taps, emit):
    blocks, rows, planes, _ = center.shape
    margin = above.shape[1]
    tiles = planes // 8
    group = 16 if rows % 16 == 0 else 8

    def column(index, _):
        block, start = index // tiles, pl.multiple_of((index % tiles) * 8, 8)

        def row(place):
            if place < 0:
                return above[block, margin + place, pl.ds(start, 8), :]
            if place < rows:
                return center[block, place, pl.ds(start, 8), :]
            return below[block, place - rows, pl.ds(start, 8), :]

        for first in range(0, rows, group):
            sums = [None] * group
            for place in range(first - margin, first + group + margin):
                value = row(place)
                for slot in range(group):
                    tap = place - (first + slot) + margin
                    if 0 <= tap <= 2 * margin:
                        term = taps[tap] * value
                        sums[slot] = term if sums[slot] is None else sums[slot] + term
            for slot in range(group):
                emit(block, start, first + slot, sums[slot])
        return 0

    lax.fori_loop(0, blocks * tiles, column, 0)


def plane_loader(ref):
    blocks, _, planes, width = ref.shape
    return lambda row: ref[:, row].reshape(blocks * planes, width)


def plane_storer(ref):
    blocks, _, planes, width = ref.shape

    def store(row, value):
        ref[:, row] = value.reshape(blocks, planes, width)

    return store


def copy_ends(ref, head, tail):
    rows, kept = ref.shape[1], head.shape[1]
    head[...] = ref[:, :kept]
    tail[...] = ref[:, rows - kept :]


def blur_kernel(current, matrix_y, matrix_z, out, head, tail):
    along_yz(plane_loader(current), plane_storer(out), matrix_y[...], matrix_z[...], out.shape[1])
    copy_ends(out, head, tail)


def quotient_kernel(taps, center, above, below, data, matrix_y, matrix_z, out, head, tail, blurred):
    length = taps.shape[0]
    weights = [taps[length - 1 - k] for k in range(length)]

    def emit(block, start, row, value):
        blurred[block, row, pl.ds(start, 8), :] = value

    along_x(center, above, below, weights, emit)
    data_of, blurred_of = plane_loader(data), plane_loader(blurred)
    along_yz(
        lambda row: data_of(row) / blurred_of(row),
        plane_storer(out),
        matrix_y[...],
        matrix_z[...],
        out.shape[1],
    )
    copy_ends(out, head, tail)


def update_kernel(taps, center, above, below, current, matrix_y, matrix_z, updated, out, head, tail):
    weights = [taps[k] for k in range(taps.shape[0])]

    def emit(block, start, row, value):
        updated[block, row, pl.ds(start, 8), :] = current[block, row, pl.ds(start, 8), :] * value

    along_x(center, above, below, weights, emit)
    along_yz(plane_loader(updated), plane_storer(out), matrix_y[...], matrix_z[...], out.shape[1])
    copy_ends(out, head, tail)


def finish_kernel(taps, center, above, below, current, updated):
    weights = [taps[k] for k in range(taps.shape[0])]

    def emit(block, start, row, value):
        updated[block, row, pl.ds(start, 8), :] = current[block, row, pl.ds(start, 8), :] * value

    along_x(center, above, below, weights, emit)


def call(kernel, name, outs, in_specs, scratch=()):
    return pl.pallas_call(
        kernel,
        out_shape=outs,
        in_specs=in_specs,
        out_specs=jax.tree.map(lambda _: WHOLE, outs),
        scratch_shapes=list(scratch),
        compiler_params=pltpu.CompilerParams(vmem_limit_bytes=VMEM_LIMIT),
        name=name,
    )


def turn_kernel(source, target):
    target[0] = jnp.swapaxes(source[...], 0, 1)


def turn_back_kernel(source, target):
    target[...] = jnp.swapaxes(source[0], 0, 1)


def to_pencils(planes, count, run):
    depth, extent, width = planes.shape
    rows = extent // count
    if depth % 8 == 0:
        blocks = pl.pallas_call(
            turn_kernel,
            grid=(count,),
            out_shape=jax.ShapeDtypeStruct((count, rows, depth, width), planes.dtype),
            in_specs=[pl.BlockSpec((depth, rows, width), lambda g: (0, position(g, run), 0))],
            out_specs=pl.BlockSpec((1, rows, depth, width), lambda g: (g, 0, 0, 0)),
            name="turn",
        )(planes)
        return lax.all_to_all(blocks, "slab", split_axis=0, concat_axis=0, tiled=True)
    order = device_order(count, run)
    blocks = planes.reshape(depth, count, rows, width).transpose(1, 0, 2, 3)
    blocks = jnp.stack([blocks[order.index(d)] for d in range(count)])
    blocks = lax.all_to_all(blocks, "slab", split_axis=0, concat_axis=0, tiled=True)
    return blocks.reshape(1, count * depth, rows, width).swapaxes(1, 2)


def to_planes(pencils, count, run, depth):
    rows, width = pencils.shape[1], pencils.shape[3]
    if depth % 8 == 0:
        blocks = lax.all_to_all(pencils, "slab", split_axis=0, concat_axis=0, tiled=True)
        return pl.pallas_call(
            turn_back_kernel,
            grid=(count,),
            out_shape=jax.ShapeDtypeStruct((depth, rows * count, width), pencils.dtype),
            in_specs=[pl.BlockSpec((1, rows, depth, width), lambda g: (g, 0, 0, 0))],
            out_specs=pl.BlockSpec((depth, rows, width), lambda g: (0, position(g, run), 0)),
            name="turn_back",
        )(blocks)
    order = device_order(count, run)
    blocks = pencils.swapaxes(1, 2).reshape(count, depth, rows, width)
    blocks = lax.all_to_all(blocks, "slab", split_axis=0, concat_axis=0, tiled=True)
    blocks = jnp.stack([blocks[d] for d in order])
    return blocks.transpose(1, 0, 2, 3).reshape(depth, rows * count, width)


def halos(head, tail, margin, count, run):
    order = device_order(count, run)
    rows = head.shape[1]
    above, below, need, hop = [], [], margin, 1
    while need > 0:
        size = min(rows, need)
        forth = [(order[p], order[p + hop]) for p in range(count - hop)]
        back = [(order[p + hop], order[p]) for p in range(count - hop)]
        above.insert(0, lax.ppermute(tail[:, rows - size :], "slab", forth))
        below.append(lax.ppermute(head[:, :size], "slab", back))
        need, hop = need - size, hop + 1
    if len(above) == 1:
        return above[0], below[0]
    return jnp.concatenate(above, axis=1), jnp.concatenate(below, axis=1)


def body(estimate, recorded, lateral, axial_taps):
    count = lax.axis_size("slab")
    run = max(count // 4, 1)
    depth = estimate.shape[0]
    views, margin = recorded.shape[0], lateral.shape[2] // 2

    current = to_pencils(estimate, count, run)
    data = [to_pencils(recorded[v], count, run) for v in range(views)]
    blocks, rows, planes, width = current.shape
    taps = [normalized(lateral[v, 0]) for v in range(views)]
    columns = [banded(normalized(lateral[v, 1]), width) for v in range(views)]
    depths = [banded(normalized(axial_taps[v]), blocks * planes) for v in range(views)]

    volume = jax.ShapeDtypeStruct(current.shape, jnp.float32)
    end = jax.ShapeDtypeStruct((blocks, min(margin, rows), planes, width), jnp.float32)
    held = pltpu.VMEM(current.shape, jnp.float32)
    blur = call(blur_kernel, "blur", (volume, end, end), [WHOLE] * 3)
    quotient = call(quotient_kernel, "quotient", (volume, end, end), [SCALARS] + [WHOLE] * 6, [held])
    update = call(update_kernel, "update", (volume, volume, end, end), [SCALARS] + [WHOLE] * 6)
    finish = call(finish_kernel, "finish", volume, [SCALARS] + [WHOLE] * 4)

    center, head, tail = blur(current, columns[0], depths[0].T)
    for v in range(views):
        above, below = halos(head, tail, margin, count, run)
        center, head, tail = quotient(taps[v], center, above, below, data[v], columns[v].T, depths[v])
        above, below = halos(head, tail, margin, count, run)
        if v + 1 < views:
            current, center, head, tail = update(
                taps[v], center, above, below, current, columns[v + 1], depths[v + 1].T
            )
        else:
            current = finish(taps[v], center, above, below, current)
    return to_planes(current, count, run, depth)


def solution(mesh):
    in_specs = (P("slab", "groups", None), P(None, "slab", "groups", None), P(), P())
    out_specs = P("slab", "groups", None)
    return jax.shard_map(body, mesh=mesh, in_specs=in_specs, out_specs=out_specs, check_vma=False)
```

```python
import functools

import jax
import jax.numpy as jnp
from jax import lax
from jax.experimental import pallas as pl
from jax.experimental.pallas import tpu as pltpu
from jax.sharding import PartitionSpec as P

VMEM_LIMIT = 56 * 1024 * 1024
WHOLE = pl.BlockSpec(memory_space=pltpu.VMEM)
SCALARS = pl.BlockSpec(memory_space=pltpu.SMEM)
ANYWHERE = pl.BlockSpec(memory_space=pl.ANY)
TURN_US = 4


def cost(microseconds):
    return pl.CostEstimate(flops=0, bytes_accessed=int(microseconds * 3.6e6), transcendentals=0)


def banded(kernel, extent):
    length = kernel.shape[0]
    margin = length // 2
    places = jnp.arange(extent, dtype=jnp.int32)
    offsets = places[None, :] - places[:, None] + margin
    stencil = jnp.arange(length, dtype=jnp.int32)
    picked = (offsets[None, :, :] == stencil[:, None, None]).astype(jnp.float32)
    return jnp.sum(kernel[:, None, None] * picked, axis=0)


def normalized(kernel):
    return kernel / jnp.sum(kernel)


def halves(value):
    high = value.astype(jnp.bfloat16)
    low = (value - high.astype(jnp.float32)).astype(jnp.bfloat16)
    return high, low


def position(device, run):
    row, place = device // run, device % run
    return row * run + jnp.where(row % 2 == 0, place, run - 1 - place)


def device_order(count, run):
    return [r * run + (p if r % 2 == 0 else run - 1 - p) for r in range(count // run) for p in range(run)]


def along_yz(load, store, matrix_y, matrix_z, rows):
    depth, width = matrix_z.shape[0], matrix_y.shape[0]
    right_high, right_low = halves(matrix_y)
    right = jnp.concatenate([right_high, right_low], axis=1)
    right = jnp.concatenate([right, right], axis=0)
    left_high, left_low = halves(matrix_z)
    left = jnp.concatenate([left_high, left_low], axis=0)
    left = jnp.concatenate([left, left], axis=1)

    def pair(index, _):
        row = 2 * index
        planes = jnp.concatenate([load(row), load(row + 1)], axis=0)
        product = jnp.dot(
            jnp.concatenate(halves(planes), axis=1), right, preferred_element_type=jnp.float32
        )
        mixed = product[:, :width] + product[:, width:]
        sides = jnp.concatenate([mixed[:depth], mixed[depth:]], axis=1)
        product = jnp.dot(
            left, jnp.concatenate(halves(sides), axis=0), preferred_element_type=jnp.float32
        )
        mixed = product[:depth] + product[depth:]
        store(row, mixed[:, :width])
        store(row + 1, mixed[:, width:])
        return 0

    lax.fori_loop(0, rows // 2, pair, 0, unroll=4)


def along_x(center, above, below, taps, emit):
    blocks, rows, planes, _ = center.shape
    margin = above.shape[1]
    tiles = planes // 8
    group = 16 if rows % 16 == 0 else 8

    def column(index, _):
        block, start = index // tiles, pl.multiple_of((index % tiles) * 8, 8)

        def row(place):
            if place < 0:
                return above[block, margin + place, pl.ds(start, 8), :]
            if place < rows:
                return center[block, place, pl.ds(start, 8), :]
            return below[block, place - rows, pl.ds(start, 8), :]

        for first in range(0, rows, group):
            sums = [None] * group
            for place in range(first - margin, first + group + margin):
                value = row(place)
                for slot in range(group):
                    tap = place - (first + slot) + margin
                    if 0 <= tap <= 2 * margin:
                        term = taps[tap] * value
                        sums[slot] = term if sums[slot] is None else sums[slot] + term
            for slot in range(group):
                emit(block, start, first + slot, sums[slot])
        return 0

    lax.fori_loop(0, blocks * tiles, column, 0)


def plane_loader(ref):
    blocks, _, planes, width = ref.shape
    return lambda row: ref[:, row].reshape(blocks * planes, width)


def plane_storer(ref):
    blocks, _, planes, width = ref.shape

    def store(row, value):
        ref[:, row] = value.reshape(blocks, planes, width)

    return store


def copy_ends(ref, head, tail):
    rows, kept = ref.shape[1], head.shape[1]
    head[...] = ref[:, :kept]
    tail[...] = ref[:, rows - kept :]


def blur_kernel(current, matrix_y, matrix_z, out, head, tail):
    along_yz(plane_loader(current), plane_storer(out), matrix_y[...], matrix_z[...], out.shape[1])
    copy_ends(out, head, tail)


def quotient_kernel(taps, center, above, below, matrix_y, matrix_z, *rest):
    parts, (out, head, tail, blurred) = rest[:-4], rest[-4:]
    length = taps.shape[0]
    weights = [taps[length - 1 - k] for k in range(length)]

    def emit(block, start, row, value):
        blurred[block, row, pl.ds(start, 8), :] = value

    along_x(center, above, below, weights, emit)
    blurred_of, store = plane_loader(blurred), plane_storer(out)
    begin = 0
    for data in parts:
        data_of = plane_loader(data)
        along_yz(
            lambda row: data_of(row) / blurred_of(begin + row),
            lambda row, value: store(begin + row, value),
            matrix_y[...],
            matrix_z[...],
            data.shape[1],
        )
        begin += data.shape[1]
    copy_ends(out, head, tail)


def update_kernel(taps, center, above, below, current, matrix_y, matrix_z, arrived, updated, out, head, tail):
    weights = [taps[k] for k in range(taps.shape[0])]

    def emit(block, start, row, value):
        updated[block, row, pl.ds(start, 8), :] = current[block, row, pl.ds(start, 8), :] * value

    along_x(center, above, below, weights, emit)
    along_yz(plane_loader(updated), plane_storer(out), matrix_y[...], matrix_z[...], out.shape[1])
    copy_ends(out, head, tail)


def finish_kernel(taps, center, above, below, current, updated):
    weights = [taps[k] for k in range(taps.shape[0])]

    def emit(block, start, row, value):
        updated[block, row, pl.ds(start, 8), :] = current[block, row, pl.ds(start, 8), :] * value

    along_x(center, above, below, weights, emit)


def call(kernel, name, microseconds, outs, in_specs, scratch=()):
    return pl.pallas_call(
        kernel,
        out_shape=outs,
        in_specs=in_specs,
        out_specs=jax.tree.map(lambda _: WHOLE, outs),
        scratch_shapes=list(scratch),
        compiler_params=pltpu.CompilerParams(vmem_limit_bytes=VMEM_LIMIT),
        cost_estimate=cost(microseconds),
        name=name,
    )


def turn_kernel(source, *rest):
    target = rest[-1]
    depth, rows, width = source.shape
    flat = source.reshape(depth * rows, width)
    for row in range(rows):
        target[0, row] = flat[pl.ds(row, depth, stride=rows), :]


def turn_back_kernel(source, target):
    _, rows, depth, width = source.shape
    flat = source.reshape(rows * depth, width)
    for plane in range(depth):
        for row in range(0, rows, 8):
            target[plane, row : row + 8, :] = flat[pl.ds(row * depth + plane, 8, stride=depth), :]


def gate(blocks, arrays):
    return pl.pallas_call(
        lambda *refs: None,
        out_shape=jax.ShapeDtypeStruct(blocks.shape, blocks.dtype),
        in_specs=[ANYWHERE] * (1 + len(arrays)),
        out_specs=ANYWHERE,
        input_output_aliases={0: 0},
        cost_estimate=cost(0.5),
        name="gate",
    )(blocks, *arrays)


def to_pencils(planes, count, run, part=0, parts=1, turn_after=(), send_after=()):
    depth, extent, width = planes.shape
    rows = extent // count // parts
    if depth % 8 == 0:
        blocks = pl.pallas_call(
            turn_kernel,
            grid=(count,),
            out_shape=jax.ShapeDtypeStruct((count, rows, depth, width), planes.dtype),
            in_specs=[pl.BlockSpec((depth, rows, width), lambda g: (0, position(g, run) * parts + part, 0))]
            + [ANYWHERE] * len(turn_after),
            out_specs=pl.BlockSpec((1, rows, depth, width), lambda g: (g, 0, 0, 0)),
            cost_estimate=cost(TURN_US / parts),
            name="turn",
        )(planes, *turn_after)
        if send_after:
            blocks = gate(blocks, send_after)
        return lax.all_to_all(blocks, "slab", split_axis=0, concat_axis=0, tiled=True)
    order = device_order(count, run)
    blocks = planes.reshape(depth, count, parts, rows, width)[:, :, part].transpose(1, 0, 2, 3)
    blocks = jnp.stack([blocks[order.index(d)] for d in range(count)])
    blocks = lax.all_to_all(blocks, "slab", split_axis=0, concat_axis=0, tiled=True)
    return blocks.reshape(1, count * depth, rows, width).swapaxes(1, 2)


def to_planes(pencils, count, run, depth):
    rows, width = pencils.shape[1], pencils.shape[3]
    if depth % 8 == 0:
        blocks = lax.all_to_all(pencils, "slab", split_axis=0, concat_axis=0, tiled=True)
        return pl.pallas_call(
            turn_back_kernel,
            grid=(count,),
            out_shape=jax.ShapeDtypeStruct((depth, rows * count, width), pencils.dtype),
            in_specs=[pl.BlockSpec((1, rows, depth, width), lambda g: (g, 0, 0, 0))],
            out_specs=pl.BlockSpec((depth, rows, width), lambda g: (0, position(g, run), 0)),
            cost_estimate=cost(TURN_US),
            name="turn_back",
        )(blocks)
    order = device_order(count, run)
    blocks = pencils.swapaxes(1, 2).reshape(count, depth, rows, width)
    blocks = lax.all_to_all(blocks, "slab", split_axis=0, concat_axis=0, tiled=True)
    blocks = jnp.stack([blocks[d] for d in order])
    return blocks.transpose(1, 0, 2, 3).reshape(depth, rows * count, width)


def halos(head, tail, margin, count, run):
    order = device_order(count, run)
    rows = head.shape[1]
    above, below, need, hop = [], [], margin, 1
    while need > 0:
        size = min(rows, need)
        forth = [(order[p], order[p + hop]) for p in range(count - hop)]
        back = [(order[p + hop], order[p]) for p in range(count - hop)]
        above.insert(0, lax.ppermute(tail[:, rows - size :], "slab", forth))
        below.append(lax.ppermute(head[:, :size], "slab", back))
        need, hop = need - size, hop + 1
    if len(above) == 1:
        return above[0], below[0]
    return jnp.concatenate(above, axis=1), jnp.concatenate(below, axis=1)


def body(estimate, recorded, lateral, axial_taps):
    count = lax.axis_size("slab")
    run = max(count // 4, 1)
    depth = estimate.shape[0]
    views, margin = recorded.shape[0], lateral.shape[2] // 2

    current = to_pencils(estimate, count, run)
    blocks, rows, planes, width = current.shape
    taps = [normalized(lateral[v, 0]) for v in range(views)]
    columns = [banded(normalized(lateral[v, 1]), width) for v in range(views)]
    depths = [banded(normalized(axial_taps[v]), blocks * planes) for v in range(views)]

    volume = jax.ShapeDtypeStruct(current.shape, jnp.float32)
    end = jax.ShapeDtypeStruct((blocks, min(margin, rows), planes, width), jnp.float32)
    held = pltpu.VMEM(current.shape, jnp.float32)
    blur = call(blur_kernel, "blur", 10, (volume, end, end), [WHOLE] * 3)
    def quotient(pieces):
        specs = [SCALARS] + [WHOLE] * (5 + pieces)
        return call(quotient_kernel, "quotient", 20, (volume, end, end), specs, [held])

    update = call(
        update_kernel, "update", 21, (volume, volume, end, end), [SCALARS] + [WHOLE] * 6 + [ANYWHERE]
    )
    finish = call(finish_kernel, "finish", 15, volume, [SCALARS] + [WHOLE] * 4)

    parts = [to_pencils(recorded[0], count, run)]
    center, head, tail = blur(current, columns[0], depths[0].T)
    for v in range(views):
        above, below = halos(head, tail, margin, count, run)
        coming = [] if v + 1 == views else [to_pencils(recorded[v + 1], count, run, 0, 2, (head,), (above, below))]
        center, head, tail = quotient(len(parts))(
            taps[v], center, above, below, columns[v].T, depths[v], *parts
        )
        above, below = halos(head, tail, margin, count, run)
        if v + 1 < views:
            coming.append(to_pencils(recorded[v + 1], count, run, 1, 2, (head,), (above, below)))
            current, center, head, tail = update(
                taps[v], center, above, below, current, columns[v + 1], depths[v + 1].T, coming[0]
            )
            parts = coming
        else:
            current = finish(taps[v], center, above, below, current)
    return to_planes(current, count, run, depth)


def solution(mesh):
    in_specs = (P("slab", "groups", None), P(None, "slab", "groups", None), P(), P())
    out_specs = P("slab", "groups", None)
    return jax.shard_map(body, mesh=mesh, in_specs=in_specs, out_specs=out_specs, check_vma=False)
```

```python
import functools

import jax
import jax.numpy as jnp
from jax import lax
from jax.experimental import pallas as pl
from jax.experimental.pallas import tpu as pltpu
from jax.sharding import PartitionSpec as P

VMEM_LIMIT = 56 * 1024 * 1024
WHOLE = pl.BlockSpec(memory_space=pltpu.VMEM)
SCALARS = pl.BlockSpec(memory_space=pltpu.SMEM)
ANYWHERE = pl.BlockSpec(memory_space=pl.ANY)
TURN_US = 4


def cost(microseconds):
    return pl.CostEstimate(flops=0, bytes_accessed=int(microseconds * 3.6e6), transcendentals=0)


def banded(kernel, extent):
    length = kernel.shape[0]
    margin = length // 2
    places = jnp.arange(extent, dtype=jnp.int32)
    offsets = places[None, :] - places[:, None] + margin
    stencil = jnp.arange(length, dtype=jnp.int32)
    picked = (offsets[None, :, :] == stencil[:, None, None]).astype(jnp.float32)
    return jnp.sum(kernel[:, None, None] * picked, axis=0)


def normalized(kernel):
    return kernel / jnp.sum(kernel)


def halves(value):
    high = value.astype(jnp.bfloat16)
    low = (value - high.astype(jnp.float32)).astype(jnp.bfloat16)
    return high, low


def position(device, run):
    row, place = device // run, device % run
    return row * run + jnp.where(row % 2 == 0, place, run - 1 - place)


def device_order(count, run):
    return [r * run + (p if r % 2 == 0 else run - 1 - p) for r in range(count // run) for p in range(run)]


def along_yz(load, store, matrix_y, matrix_z, rows):
    depth, width = matrix_z.shape[0], matrix_y.shape[0]
    right_high, right_low = halves(matrix_y)
    right = jnp.concatenate([right_high, right_low], axis=1)
    right = jnp.concatenate([right, right], axis=0)
    left_high, left_low = halves(matrix_z)
    left = jnp.concatenate([left_high, left_low], axis=0)
    left = jnp.concatenate([left, left], axis=1)

    def pair(index, _):
        row = 2 * index
        planes = jnp.concatenate([load(row), load(row + 1)], axis=0)
        product = jnp.dot(
            jnp.concatenate(halves(planes), axis=1), right, preferred_element_type=jnp.float32
        )
        mixed = product[:, :width] + product[:, width:]
        sides = jnp.concatenate([mixed[:depth], mixed[depth:]], axis=1)
        product = jnp.dot(
            left, jnp.concatenate(halves(sides), axis=0), preferred_element_type=jnp.float32
        )
        mixed = product[:depth] + product[depth:]
        store(row, mixed[:, :width])
        store(row + 1, mixed[:, width:])
        return 0

    lax.fori_loop(0, rows // 2, pair, 0, unroll=4)


def find(pieces, row):
    for piece in pieces:
        if row < piece.shape[1]:
            return piece, row
        row -= piece.shape[1]


def along_x(pieces, above, below, taps, emit):
    blocks, _, planes, _ = pieces[0].shape
    rows = sum(piece.shape[1] for piece in pieces)
    margin = above.shape[1]
    tiles = planes // 8
    group = 16 if rows % 16 == 0 else 8

    def column(index, _):
        block, start = index // tiles, pl.multiple_of((index % tiles) * 8, 8)

        def row(place):
            if place < 0:
                return above[block, margin + place, pl.ds(start, 8), :]
            if place < rows:
                piece, inside = find(pieces, place)
                return piece[block, inside, pl.ds(start, 8), :]
            return below[block, place - rows, pl.ds(start, 8), :]

        for first in range(0, rows, group):
            sums = [None] * group
            for place in range(first - margin, first + group + margin):
                value = row(place)
                for slot in range(group):
                    tap = place - (first + slot) + margin
                    if 0 <= tap <= 2 * margin:
                        term = taps[tap] * value
                        sums[slot] = term if sums[slot] is None else sums[slot] + term
            for slot in range(group):
                emit(block, start, first + slot, sums[slot])
        return 0

    lax.fori_loop(0, blocks * tiles, column, 0)


def plane_loader(ref):
    blocks, _, planes, width = ref.shape
    return lambda row: ref[:, row].reshape(blocks * planes, width)


def plane_storer(ref):
    blocks, _, planes, width = ref.shape

    def store(row, value):
        ref[:, row] = value.reshape(blocks, planes, width)

    return store


def copy_ends(ref, head, tail):
    rows, kept = ref.shape[1], head.shape[1]
    head[...] = ref[:, :kept]
    tail[...] = ref[:, rows - kept :]


def blur_kernel(current, matrix_y, matrix_z, out, head, tail):
    along_yz(plane_loader(current), plane_storer(out), matrix_y[...], matrix_z[...], out.shape[1])
    copy_ends(out, head, tail)


def quotient_kernel(taps, center, above, below, matrix_y, matrix_z, *rest):
    parts, (out, head, tail, blurred) = rest[:-4], rest[-4:]
    length = taps.shape[0]
    weights = [taps[length - 1 - k] for k in range(length)]

    def emit(block, start, row, value):
        blurred[block, row, pl.ds(start, 8), :] = value

    along_x([center], above, below, weights, emit)
    blurred_of, store = plane_loader(blurred), plane_storer(out)
    begin = 0
    for data in parts:
        data_of = plane_loader(data)
        along_yz(
            lambda row: data_of(row) / blurred_of(begin + row),
            lambda row, value: store(begin + row, value),
            matrix_y[...],
            matrix_z[...],
            data.shape[1],
        )
        begin += data.shape[1]
    copy_ends(out, head, tail)


def update_kernel(taps, center, above, below, current, matrix_y, matrix_z, arrived, updated, out, head, tail):
    weights = [taps[k] for k in range(taps.shape[0])]

    def emit(block, start, row, value):
        updated[block, row, pl.ds(start, 8), :] = current[block, row, pl.ds(start, 8), :] * value

    along_x([center], above, below, weights, emit)
    along_yz(plane_loader(updated), plane_storer(out), matrix_y[...], matrix_z[...], out.shape[1])
    copy_ends(out, head, tail)


def finish_kernel(count, taps, above, below, current, *rest):
    pieces, updated = rest[:count], rest[count]
    weights = [taps[k] for k in range(taps.shape[0])]

    def emit(block, start, row, value):
        updated[block, row, pl.ds(start, 8), :] = current[block, row, pl.ds(start, 8), :] * value

    along_x(pieces, above, below, weights, emit)


def lines_kernel(taps, center, above, below, *pieces):
    length = taps.shape[0]
    weights = [taps[length - 1 - k] for k in range(length)]

    def emit(block, start, row, value):
        piece, inside = find(pieces, row)
        piece[block, inside, pl.ds(start, 8), :] = value

    along_x([center], above, below, weights, emit)


def edges_kernel(blurred_0, blurred_1, data_0, data_1, matrix_y, matrix_z, out_0, out_1, head, tail):
    for blurred, data, out in ((blurred_0, data_0, out_0), (blurred_1, data_1, out_1)):
        divide_kernel(blurred, data, matrix_y, matrix_z, out)
    rows, kept = out_1.shape[1], head.shape[1]
    head[...] = out_0[:, :kept]
    tail[...] = out_1[:, rows - kept :]


def divide_kernel(blurred, data, matrix_y, matrix_z, out):
    data_of, blurred_of = plane_loader(data), plane_loader(blurred)
    along_yz(
        lambda row: data_of(row) / blurred_of(row),
        plane_storer(out),
        matrix_y[...],
        matrix_z[...],
        out.shape[1],
    )


def striped(kernel, name, microseconds, inputs, outs):
    def spec(array):
        step = 2 if array.shape[0] % 2 == 0 else 1
        return pl.BlockSpec((step,) + array.shape[1:], lambda g: (g, 0, 0, 0))

    blocks = outs[0].shape[0]
    return pl.pallas_call(
        kernel,
        grid=(blocks // 2 if blocks % 2 == 0 else blocks,),
        out_shape=outs,
        in_specs=[SCALARS] + [spec(array) for array in inputs[1:]],
        out_specs=[spec(array) for array in outs],
        compiler_params=pltpu.CompilerParams(vmem_limit_bytes=VMEM_LIMIT),
        cost_estimate=cost(microseconds),
        name=name,
    )(*inputs)


def call(kernel, name, microseconds, outs, in_specs, scratch=()):
    return pl.pallas_call(
        kernel,
        out_shape=outs,
        in_specs=in_specs,
        out_specs=jax.tree.map(lambda _: WHOLE, outs),
        scratch_shapes=list(scratch),
        compiler_params=pltpu.CompilerParams(vmem_limit_bytes=VMEM_LIMIT),
        cost_estimate=cost(microseconds),
        name=name,
    )


def source_block(place, run):
    return jnp.where(pl.program_id(0) % 2 == 0, place, run - 1 - place)


def turn_kernel(run, begin, source, *rest):
    target = rest[-1]
    depth, extent, width = source.shape
    flat = source.reshape(depth * extent, width)
    for place in range(run):
        base = source_block(place, run) * (extent // run) + begin
        for row in range(target.shape[1]):
            target[place, row] = flat[pl.ds(base + row, depth, stride=extent), :]


def turn_back_kernel(run, source, target):
    _, rows, depth, width = source.shape
    flat = source.reshape(run * rows * depth, width)
    for place in range(run):
        base = source_block(place, run) * rows
        for plane in range(depth):
            for row in range(0, rows, 8):
                target[plane, pl.ds(pl.multiple_of(base + row, 8), 8), :] = flat[
                    pl.ds((place * rows + row) * depth + plane, 8, stride=depth), :
                ]


def gate(blocks, arrays):
    return pl.pallas_call(
        lambda *refs: None,
        out_shape=jax.ShapeDtypeStruct(blocks.shape, blocks.dtype),
        in_specs=[ANYWHERE] * (1 + len(arrays)),
        out_specs=ANYWHERE,
        input_output_aliases={0: 0},
        cost_estimate=cost(0.5),
        name="gate",
    )(blocks, *arrays)


def to_pencils(planes, count, run, begin=0, size=None, turn_after=(), send_after=()):
    depth, extent, width = planes.shape
    rows = extent // count
    size = rows if size is None else size
    if depth % 8 == 0 and rows % 8 == 0:
        blocks = pl.pallas_call(
            functools.partial(turn_kernel, run, begin),
            grid=(count // run,),
            out_shape=jax.ShapeDtypeStruct((count, size, depth, width), planes.dtype),
            in_specs=[pl.BlockSpec((depth, run * rows, width), lambda g: (0, g, 0))]
            + [ANYWHERE] * len(turn_after),
            out_specs=pl.BlockSpec((run, size, depth, width), lambda g: (g, 0, 0, 0)),
            compiler_params=pltpu.CompilerParams(vmem_limit_bytes=VMEM_LIMIT),
            cost_estimate=cost(TURN_US),
            name="turn",
        )(planes, *turn_after)
        if send_after:
            blocks = gate(blocks, send_after)
        return lax.all_to_all(blocks, "slab", split_axis=0, concat_axis=0, tiled=True)
    order = device_order(count, run)
    blocks = planes.reshape(depth, count, rows, width)[:, :, begin : begin + size].transpose(1, 0, 2, 3)
    blocks = jnp.stack([blocks[order.index(d)] for d in range(count)])
    blocks = lax.all_to_all(blocks, "slab", split_axis=0, concat_axis=0, tiled=True)
    return blocks.reshape(1, count * depth, size, width).swapaxes(1, 2)


def to_planes(pencils, count, run, depth):
    rows, width = pencils.shape[1], pencils.shape[3]
    if depth % 8 == 0 and rows % 8 == 0:
        blocks = lax.all_to_all(pencils, "slab", split_axis=0, concat_axis=0, tiled=True)
        return pl.pallas_call(
            functools.partial(turn_back_kernel, run),
            grid=(count // run,),
            out_shape=jax.ShapeDtypeStruct((depth, rows * count, width), pencils.dtype),
            in_specs=[pl.BlockSpec((run, rows, depth, width), lambda g: (g, 0, 0, 0))],
            out_specs=pl.BlockSpec((depth, run * rows, width), lambda g: (0, g, 0)),
            compiler_params=pltpu.CompilerParams(vmem_limit_bytes=VMEM_LIMIT),
            cost_estimate=cost(TURN_US),
            name="turn_back",
        )(blocks)
    order = device_order(count, run)
    blocks = pencils.swapaxes(1, 2).reshape(count, depth, rows, width)
    blocks = lax.all_to_all(blocks, "slab", split_axis=0, concat_axis=0, tiled=True)
    blocks = jnp.stack([blocks[d] for d in order])
    return blocks.transpose(1, 0, 2, 3).reshape(depth, rows * count, width)


def halos(head, tail, margin, count, run):
    order = device_order(count, run)
    rows = head.shape[1]
    above, below, need, hop = [], [], margin, 1
    while need > 0:
        size = min(rows, need)
        forth = [(order[p], order[p + hop]) for p in range(count - hop)]
        back = [(order[p + hop], order[p]) for p in range(count - hop)]
        above.insert(0, lax.ppermute(tail[:, rows - size :], "slab", forth))
        below.append(lax.ppermute(head[:, :size], "slab", back))
        need, hop = need - size, hop + 1
    if len(above) == 1:
        return above[0], below[0]
    return jnp.concatenate(above, axis=1), jnp.concatenate(below, axis=1)


def body(estimate, recorded, lateral, axial_taps):
    count = lax.axis_size("slab")
    run = max(count // 4, 1)
    depth = estimate.shape[0]
    views, margin = recorded.shape[0], lateral.shape[2] // 2

    current = to_pencils(estimate, count, run)
    blocks, rows, planes, width = current.shape
    taps = [normalized(lateral[v, 0]) for v in range(views)]
    columns = [banded(normalized(lateral[v, 1]), width) for v in range(views)]
    depths = [banded(normalized(axial_taps[v]), blocks * planes) for v in range(views)]

    volume = jax.ShapeDtypeStruct(current.shape, jnp.float32)
    end = jax.ShapeDtypeStruct((blocks, min(margin, rows), planes, width), jnp.float32)
    held = pltpu.VMEM(current.shape, jnp.float32)
    blur = call(blur_kernel, "blur", 10, (volume, end, end), [WHOLE] * 3)
    def quotient(pieces):
        specs = [SCALARS] + [WHOLE] * (5 + pieces)
        return call(quotient_kernel, "quotient", 20, (volume, end, end), specs, [held])

    update = call(
        update_kernel, "update", 21, (volume, volume, end, end), [SCALARS] + [WHOLE] * 6 + [ANYWHERE]
    )

    def send(v, begin, size, turn_after=(), send_after=()):
        return to_pencils(recorded[v], count, run, begin, size, turn_after, send_after)

    half, last = rows // 2, views - 1
    outer = 3 * rows // 8 if rows % 16 == 0 else 0
    split_last = outer >= margin + 1 and views > 1
    parts = [send(0, 0, rows)]
    center, head, tail = blur(current, columns[0], depths[0].T)
    for v in range(views):
        above, below = halos(head, tail, margin, count, run)
        if v == last and split_last:
            middle = send(v, outer, rows - 2 * outer, (head,), (above, below))
            sizes = (outer, rows - 2 * outer, outer)
            pieces = [jax.ShapeDtypeStruct((blocks, size, planes, width), jnp.float32) for size in sizes]
            blurred = striped(lines_kernel, "lines", 11, [taps[v], center, above, below], pieces)
            first, second, head, tail = call(
                edges_kernel, "edges", 8, (pieces[0], pieces[2], end, end), [WHOLE] * 6
            )(blurred[0], blurred[2], *parts, columns[v].T, depths[v])
            above, below = halos(head, tail, margin, count, run)
            inner = call(divide_kernel, "middle", 3, pieces[1], [WHOLE] * 4)(
                blurred[1], middle, columns[v].T, depths[v]
            )
            pieces = [first, inner, second]
        else:
            coming = []
            ahead = outer if v + 1 == last and split_last else half
            if v < last:
                coming.append(send(v + 1, 0, ahead, (head,), (above, below)))
            center, head, tail = quotient(len(parts))(
                taps[v], center, above, below, columns[v].T, depths[v], *parts
            )
            above, below = halos(head, tail, margin, count, run)
            if v < last:
                coming.append(send(v + 1, rows - ahead, ahead, (head,), (above, below)))
                current, center, head, tail = update(
                    taps[v], center, above, below, current, columns[v + 1], depths[v + 1].T, coming[0]
                )
                parts = coming
            pieces = [center]
    (current,) = striped(
        functools.partial(finish_kernel, len(pieces)),
        "finish",
        11,
        [taps[last], above, below, current, *pieces],
        [volume],
    )
    return to_planes(current, count, run, depth)


def solution(mesh):
    in_specs = (P("slab", "groups", None), P(None, "slab", "groups", None), P(), P())
    out_specs = P("slab", "groups", None)
    return jax.shard_map(body, mesh=mesh, in_specs=in_specs, out_specs=out_specs, check_vma=False)
```

```python
import functools

import jax
import jax.numpy as jnp
import numpy as np
from jax import lax
from jax.experimental import pallas as pl
from jax.experimental.pallas import tpu as pltpu
from jax.sharding import PartitionSpec as P

VMEM_LIMIT = 56 * 1024 * 1024
WHOLE = pl.BlockSpec(memory_space=pltpu.VMEM)
ANYWHERE = pl.BlockSpec(memory_space=pl.ANY)
TURN_US = 4


def cost(microseconds):
    return pl.CostEstimate(flops=0, bytes_accessed=int(microseconds * 3.6e6), transcendentals=0)


def banded(kernel, extent):
    length = kernel.shape[0]
    margin = length // 2
    places = jnp.arange(extent, dtype=jnp.int32)
    offsets = places[None, :] - places[:, None] + margin
    stencil = jnp.arange(length, dtype=jnp.int32)
    picked = (offsets[None, :, :] == stencil[:, None, None]).astype(jnp.float32)
    return jnp.sum(kernel[:, None, None] * picked, axis=0)


def normalized(kernel):
    return kernel / jnp.sum(kernel)


def halves(value):
    high = value.astype(jnp.bfloat16)
    low = (value - high.astype(jnp.float32)).astype(jnp.bfloat16)
    return high, low


def position(device, run):
    row, place = device // run, device % run
    return row * run + jnp.where(row % 2 == 0, place, run - 1 - place)


def device_order(count, run):
    return [r * run + (p if r % 2 == 0 else run - 1 - p) for r in range(count // run) for p in range(run)]


def along_yz(load, store, matrix_y, matrix_z, rows):
    depth, width = matrix_z.shape[0], matrix_y.shape[0]
    right_high, right_low = halves(matrix_y)
    right = jnp.concatenate([right_high, right_low], axis=1)
    right = jnp.concatenate([right, right], axis=0)
    left_high, left_low = halves(matrix_z)
    left = jnp.concatenate([left_high, left_low], axis=0)
    left = jnp.concatenate([left, left], axis=1)

    def pair(index, _):
        row = 2 * index
        planes = jnp.concatenate([load(row), load(row + 1)], axis=0)
        product = jnp.dot(
            jnp.concatenate(halves(planes), axis=1), right, preferred_element_type=jnp.float32
        )
        mixed = product[:, :width] + product[:, width:]
        sides = jnp.concatenate([mixed[:depth], mixed[depth:]], axis=1)
        product = jnp.dot(
            left, jnp.concatenate(halves(sides), axis=0), preferred_element_type=jnp.float32
        )
        mixed = product[:depth] + product[depth:]
        store(row, mixed[:, :width])
        store(row + 1, mixed[:, width:])
        return 0

    lax.fori_loop(0, rows // 2, pair, 0, unroll=4)


def x_plane(ref, block, plane):
    blocks, rows, planes, width = ref.shape
    flat = ref.reshape(blocks * rows * planes, width)
    return flat[pl.ds(block * rows * planes + plane, rows, stride=planes), :]


def set_x_plane(ref, block, plane, value):
    blocks, rows, planes, width = ref.shape
    flat = ref.reshape(blocks * rows * planes, width)
    flat[pl.ds(block * rows * planes + plane, rows, stride=planes), :] = value


def padded(size):
    return -(-size // 16) * 16


def along_x(groups, matrix, emit):
    blocks, _, planes, width = groups[0][0].shape
    left_high, left_low = halves(matrix)
    left = jnp.concatenate([left_high, left_low], axis=0)
    left = jnp.concatenate([left, left], axis=1)

    def column(block, plane):
        parts = []
        for group in groups:
            parts += [x_plane(piece, block, plane) for piece in group]
            size = sum(piece.shape[1] for piece in group)
            if padded(size) > size:
                parts.append(jnp.zeros((padded(size) - size, width), jnp.float32))
        return jnp.concatenate(parts, axis=0)

    def pair(index, _):
        block, plane = index // (planes // 2), (index % (planes // 2)) * 2
        columns = jnp.concatenate([column(block, plane), column(block, plane + 1)], axis=1)
        product = jnp.dot(
            left, jnp.concatenate(halves(columns), axis=0), preferred_element_type=jnp.float32
        )
        mixed = product[: product.shape[0] // 2] + product[product.shape[0] // 2 :]
        emit(block, plane, mixed[:, :width])
        emit(block, plane + 1, mixed[:, width:])
        return 0

    lax.fori_loop(0, blocks * planes // 2, pair, 0, unroll=4)


def x_matrix(taps, groups, target):
    margin, nowhere = taps.shape[0] // 2, 1 << 20
    source = np.concatenate(
        [np.r_[np.arange(x, x + n), np.full(padded(n) - n, nowhere)] for x, n in groups]
    )
    rows = np.arange(padded(target[1]))
    offset = source[None, :] - (target[0] + rows)[:, None] + margin
    offset = np.where(rows[:, None] < target[1], offset, -1).astype(np.int32)
    stencil = jnp.arange(taps.shape[0], dtype=jnp.int32)
    picked = (jnp.asarray(offset)[None] == stencil[:, None, None]).astype(jnp.float32)
    return jnp.sum(taps[:, None, None] * picked, axis=0)


def plane_loader(ref):
    blocks, _, planes, width = ref.shape
    return lambda row: ref[:, row].reshape(blocks * planes, width)


def plane_storer(ref):
    blocks, _, planes, width = ref.shape

    def store(row, value):
        ref[:, row] = value.reshape(blocks, planes, width)

    return store


def copy_ends(first, second, head, tail):
    rows, kept = second.shape[1], head.shape[1]
    head[...] = first[:, :kept]
    tail[...] = second[:, rows - kept :]


def divide_yz(blurred, data, out, matrix_y, matrix_z, begin=0, place=0):
    data_of, blurred_of = plane_loader(data), plane_loader(blurred)
    along_yz(
        lambda row: data_of(place + row) / blurred_of(begin + row),
        plane_storer(out),
        matrix_y,
        matrix_z,
        out.shape[1],
    )


def blur(wide, mixed, blurred, blur_x, blur_y, blur_z):
    along_yz(plane_loader(wide), plane_storer(mixed), blur_y[...], blur_z[...], wide.shape[1])
    rows = blurred.shape[1]
    along_x([[mixed]], blur_x[...], lambda b, p, value: set_x_plane(blurred, b, p, value[:rows]))


def update(spread_x, above, center, below, before, wide):
    rows = wide.shape[1]

    def emit(block, plane, value):
        set_x_plane(wide, block, plane, x_plane(before, block, plane) * value[:rows])

    along_x([[above], [center], [below]], spread_x[...], emit)


def first_kernel(
    blur_x, blur_y, blur_z, back_y, back_z, above, own, below, data, wide, out, head, tail, mixed, blurred
):
    margin, rows = above.shape[1], own.shape[1]
    wide[:, :margin] = above[...]
    wide[:, margin : margin + rows] = own[...]
    wide[:, margin + rows : rows + 2 * margin] = below[...]
    if wide.shape[1] > rows + 2 * margin:
        wide[:, rows + 2 * margin :] = jnp.zeros_like(wide[:, rows + 2 * margin :])
    blur(wide, mixed, blurred, blur_x, blur_y, blur_z)
    divide_yz(blurred, data, out, back_y[...], back_z[...])
    copy_ends(out, out, head, tail)


def view_kernel(
    spread_x, blur_x, blur_y, blur_z, back_y, back_z, above, center, below, before, data,
    wide, out, head, tail, mixed, blurred,
):
    update(spread_x, above, center, below, before, wide)
    blur(wide, mixed, blurred, blur_x, blur_y, blur_z)
    divide_yz(blurred, data, out, back_y[...], back_z[...])
    copy_ends(out, out, head, tail)


def last_kernel(
    margin, spread_x, blur_x, blur_y, blur_z, back_y, back_z, above, center, below, before, data,
    own, inner, out_0, out_1, head, tail, wide, mixed, blurred,
):
    update(spread_x, above, center, below, before, wide)
    own[...] = wide[:, margin : margin + own.shape[1]]
    blur(wide, mixed, blurred, blur_x, blur_y, blur_z)
    outer, between = out_0.shape[1], inner.shape[1]
    inner[...] = blurred[:, outer : outer + between]
    divide_yz(blurred, data, out_0, back_y[...], back_z[...])
    divide_yz(blurred, data, out_1, back_y[...], back_z[...], outer + between, outer)
    copy_ends(out_0, out_1, head, tail)


def middle_kernel(back_y, back_z, blurred, data, out):
    divide_yz(blurred, data, out, back_y[...], back_z[...])


def finish_kernel(count, spread_x, above, below, current, *rest):
    pieces, updated = rest[:count], rest[count]
    rows = updated.shape[1]

    def emit(block, plane, value):
        set_x_plane(updated, block, plane, x_plane(current, block, plane) * value[:rows])

    along_x([[above], pieces, [below]], spread_x[...], emit)


def striped(kernel, name, microseconds, inputs, outs):
    blocks = outs[0].shape[0]
    step = 4 if blocks % 4 == 0 else 1

    def spec(array):
        return pl.BlockSpec((step,) + array.shape[1:], lambda g: (g, 0, 0, 0))

    return pl.pallas_call(
        kernel,
        grid=(blocks // step,),
        out_shape=outs,
        in_specs=[WHOLE] + [spec(array) for array in inputs[1:]],
        out_specs=[spec(array) for array in outs],
        compiler_params=pltpu.CompilerParams(vmem_limit_bytes=VMEM_LIMIT),
        cost_estimate=cost(microseconds),
        name=name,
    )(*inputs)


def call(kernel, name, microseconds, outs, in_specs, scratch=()):
    return pl.pallas_call(
        kernel,
        out_shape=outs,
        in_specs=in_specs,
        out_specs=jax.tree.map(lambda _: WHOLE, outs),
        scratch_shapes=list(scratch),
        compiler_params=pltpu.CompilerParams(vmem_limit_bytes=VMEM_LIMIT),
        cost_estimate=cost(microseconds),
        name=name,
    )


def source_block(place, run):
    return jnp.where(pl.program_id(0) % 2 == 0, place, run - 1 - place)


def turn_kernel(run, chosen, source, *rest):
    target = rest[-1]
    depth, extent, width = source.shape
    flat = source.reshape(depth * extent, width)
    for place in range(run):
        base = source_block(place, run) * (extent // run)
        for place_row, row in enumerate(chosen):
            target[place, place_row] = flat[pl.ds(base + row, depth, stride=extent), :]


def turn_back_kernel(run, source, target):
    _, rows, depth, width = source.shape
    flat = source.reshape(run * rows * depth, width)
    for place in range(run):
        base = source_block(place, run) * rows
        for plane in range(depth):
            for row in range(0, rows, 8):
                target[plane, pl.ds(pl.multiple_of(base + row, 8), 8), :] = flat[
                    pl.ds((place * rows + row) * depth + plane, 8, stride=depth), :
                ]


def gate(blocks, arrays):
    return pl.pallas_call(
        lambda *refs: None,
        out_shape=jax.ShapeDtypeStruct(blocks.shape, blocks.dtype),
        in_specs=[ANYWHERE] * (1 + len(arrays)),
        out_specs=ANYWHERE,
        input_output_aliases={0: 0},
        cost_estimate=cost(0.5),
        name="gate",
    )(blocks, *arrays)


def to_pencils(planes, count, run, chosen, turn_after=(), send_after=()):
    depth, extent, width = planes.shape
    rows = extent // count
    size = len(chosen)
    if depth % 8 == 0 and rows % 8 == 0:
        blocks = pl.pallas_call(
            functools.partial(turn_kernel, run, chosen),
            grid=(count // run,),
            out_shape=jax.ShapeDtypeStruct((count, size, depth, width), planes.dtype),
            in_specs=[pl.BlockSpec((depth, run * rows, width), lambda g: (0, g, 0))]
            + [ANYWHERE] * len(turn_after),
            out_specs=pl.BlockSpec((run, size, depth, width), lambda g: (g, 0, 0, 0)),
            compiler_params=pltpu.CompilerParams(vmem_limit_bytes=VMEM_LIMIT),
            cost_estimate=cost(TURN_US),
            name="turn",
        )(planes, *turn_after)
        if send_after:
            blocks = gate(blocks, send_after)
        return lax.all_to_all(blocks, "slab", split_axis=0, concat_axis=0, tiled=True)
    order = device_order(count, run)
    blocks = planes.reshape(depth, count, rows, width)[:, :, np.array(chosen)].transpose(1, 0, 2, 3)
    blocks = jnp.stack([blocks[order.index(d)] for d in range(count)])
    blocks = lax.all_to_all(blocks, "slab", split_axis=0, concat_axis=0, tiled=True)
    return blocks.reshape(1, count * depth, size, width).swapaxes(1, 2)


def to_planes(pencils, count, run, depth):
    rows, width = pencils.shape[1], pencils.shape[3]
    if depth % 8 == 0 and rows % 8 == 0:
        blocks = lax.all_to_all(pencils, "slab", split_axis=0, concat_axis=0, tiled=True)
        return pl.pallas_call(
            functools.partial(turn_back_kernel, run),
            grid=(count // run,),
            out_shape=jax.ShapeDtypeStruct((depth, rows * count, width), pencils.dtype),
            in_specs=[pl.BlockSpec((run, rows, depth, width), lambda g: (g, 0, 0, 0))],
            out_specs=pl.BlockSpec((depth, run * rows, width), lambda g: (0, g, 0)),
            compiler_params=pltpu.CompilerParams(vmem_limit_bytes=VMEM_LIMIT),
            cost_estimate=cost(TURN_US),
            name="turn_back",
        )(blocks)
    order = device_order(count, run)
    blocks = pencils.swapaxes(1, 2).reshape(count, depth, rows, width)
    blocks = lax.all_to_all(blocks, "slab", split_axis=0, concat_axis=0, tiled=True)
    blocks = jnp.stack([blocks[d] for d in order])
    return blocks.transpose(1, 0, 2, 3).reshape(depth, rows * count, width)


def halos(head, tail, margin, count, run):
    order = device_order(count, run)
    rows = head.shape[1]
    above, below, need, hop = [], [], margin, 1
    while need > 0:
        size = min(rows, need)
        forth = [(order[p], order[p + hop]) for p in range(count - hop)]
        back = [(order[p + hop], order[p]) for p in range(count - hop)]
        above.insert(0, lax.ppermute(tail[:, rows - size :], "slab", forth))
        below.append(lax.ppermute(head[:, :size], "slab", back))
        need, hop = need - size, hop + 1
    if len(above) == 1:
        return above[0], below[0]
    return jnp.concatenate(above, axis=1), jnp.concatenate(below, axis=1)


def body(estimate, recorded, lateral, axial_taps):
    count = lax.axis_size("slab")
    run = max(count // 4, 1)
    depth, rows, width = estimate.shape[0], estimate.shape[1] // count, estimate.shape[2]
    views, margin = recorded.shape[0], lateral.shape[2] // 2
    last = views - 1
    every = tuple(range(rows))

    current = to_pencils(estimate, count, run, every)
    data = to_pencils(recorded[0], count, run, every)
    blocks, _, planes, _ = current.shape

    def volume(size):
        return jax.ShapeDtypeStruct((blocks, size, planes, width), jnp.float32)

    def held(size):
        return pltpu.VMEM((blocks, size, planes, width), jnp.float32)

    extent, double = padded(rows + 2 * margin), 2 * margin
    end = volume(min(double, rows))
    taps = [normalized(lateral[v, 0]) for v in range(views)]
    columns = [banded(normalized(lateral[v, 1]), width) for v in range(views)]
    depths = [banded(normalized(axial_taps[v]), blocks * planes) for v in range(views)]
    blur_x = [x_matrix(t[::-1], [(-margin, extent)], (0, rows)) for t in taps]
    sides = [(-double, double), (0, rows), (rows, double)]
    spread_x = [x_matrix(t, sides, (-margin, rows + double)) for t in taps[:last]]
    sides = [(-margin, margin), (0, rows), (rows, margin)]
    finish_x = x_matrix(taps[last], sides, (0, rows))

    def matrices(v):
        return blur_x[v], columns[v], depths[v].T, columns[v].T, depths[v]

    outer = 5 * rows // 16
    split = outer >= margin + 1 and outer % 2 == 0 and views > 1
    ends = tuple(r for r in every if r < outer or r >= rows - outer)
    inside = tuple(r for r in every if outer <= r < rows - outer)

    above, below = halos(current[:, :margin], current[:, rows - margin :] if rows > margin else current, margin, count, run)
    for v in range(views):
        if v < last:
            chosen = ends if split and v + 1 == last else every
            order = (head,) if v else ()
            coming = to_pencils(recorded[v + 1], count, run, chosen, order, (above, below))
        if v == 0:
            wide, center, head, tail = call(
                first_kernel, "first", 26, (volume(extent), volume(rows), end, end), [WHOLE] * 9,
                [held(extent), held(rows)],
            )(*matrices(v), above, current, below, data)
        elif v == last and split:
            coming = to_pencils(recorded[v], count, run, inside, (head,), (above, below))
            outs = [volume(n) for n in (rows, rows - 2 * outer, outer, outer, margin, margin)]
            own, blurred, first, second, head, tail = call(
                functools.partial(last_kernel, margin), "last", 30, tuple(outs), [WHOLE] * 11,
                [held(extent), held(extent), held(rows)],
            )(spread_x[v - 1], *matrices(v), above, center, below, wide, data)
        else:
            wide, center, head, tail = call(
                view_kernel, "view", 33, (volume(extent), volume(rows), end, end), [WHOLE] * 11,
                [held(extent), held(rows)],
            )(spread_x[v - 1], *matrices(v), above, center, below, wide, data)
        reach = double
        if v == last:
            reach = margin
            head, tail = head[:, :margin], tail[:, max(tail.shape[1] - margin, 0) :]
        above, below = halos(head, tail, reach, count, run)
        data = coming
    if split:
        inner = call(middle_kernel, "middle", 3, volume(rows - 2 * outer), [WHOLE] * 4)(
            columns[last].T, depths[last], blurred, data
        )
        pieces = [first, inner, second]
    else:
        own, pieces = wide[:, margin : margin + rows], [center]
    (current,) = striped(
        functools.partial(finish_kernel, len(pieces)),
        "finish",
        8,
        [finish_x, above, below, own, *pieces],
        [volume(rows)],
    )
    return to_planes(current, count, run, depth)


def solution(mesh):
    in_specs = (P("slab", "groups", None), P(None, "slab", "groups", None), P(), P())
    out_specs = P("slab", "groups", None)
    return jax.shard_map(body, mesh=mesh, in_specs=in_specs, out_specs=out_specs, check_vma=False)
```

```python
import functools

import jax
import jax.numpy as jnp
import numpy as np
from jax import lax
from jax.experimental import pallas as pl
from jax.experimental.pallas import tpu as pltpu
from jax.sharding import PartitionSpec as P

VMEM_LIMIT = 56 * 1024 * 1024
WHOLE = pl.BlockSpec(memory_space=pltpu.VMEM)
ANYWHERE = pl.BlockSpec(memory_space=pl.ANY)
TURN_US = 4


def cost(microseconds):
    return pl.CostEstimate(flops=0, bytes_accessed=int(microseconds * 3.6e6), transcendentals=0)


def banded(kernel, extent):
    length = kernel.shape[0]
    margin = length // 2
    places = jnp.arange(extent, dtype=jnp.int32)
    offsets = places[None, :] - places[:, None] + margin
    stencil = jnp.arange(length, dtype=jnp.int32)
    picked = (offsets[None, :, :] == stencil[:, None, None]).astype(jnp.float32)
    return jnp.sum(kernel[:, None, None] * picked, axis=0)


def normalized(kernel):
    return kernel / jnp.sum(kernel)


def halves(value):
    high = value.astype(jnp.bfloat16)
    low = (value - high.astype(jnp.float32)).astype(jnp.bfloat16)
    return high, low


def position(device, run):
    row, place = device // run, device % run
    return row * run + jnp.where(row % 2 == 0, place, run - 1 - place)


def device_order(count, run):
    return [r * run + (p if r % 2 == 0 else run - 1 - p) for r in range(count // run) for p in range(run)]


def along_yz(load, store, matrix_y, matrix_z, rows):
    depth, width = matrix_z.shape[0], matrix_y.shape[0]
    right_high, right_low = halves(matrix_y)
    right = jnp.concatenate([right_high, right_low], axis=1)
    right = jnp.concatenate([right, right], axis=0)
    left_high, left_low = halves(matrix_z)
    left = jnp.concatenate([left_high, left_low], axis=0)
    left = jnp.concatenate([left, left], axis=1)

    def pair(index, _):
        row = 2 * index
        planes = jnp.concatenate([load(row), load(row + 1)], axis=0)
        product = jnp.dot(
            jnp.concatenate(halves(planes), axis=1), right, preferred_element_type=jnp.float32
        )
        mixed = product[:, :width] + product[:, width:]
        sides = jnp.concatenate([mixed[:depth], mixed[depth:]], axis=1)
        product = jnp.dot(
            left, jnp.concatenate(halves(sides), axis=0), preferred_element_type=jnp.float32
        )
        mixed = product[:depth] + product[depth:]
        store(row, mixed[:, :width])
        store(row + 1, mixed[:, width:])
        return 0

    lax.fori_loop(0, rows // 2, pair, 0, unroll=4)


def x_plane(ref, block, plane):
    blocks, rows, planes, width = ref.shape
    flat = ref.reshape(blocks * rows * planes, width)
    return flat[pl.ds(block * rows * planes + plane, rows, stride=planes), :]


def set_x_plane(ref, block, plane, value):
    blocks, rows, planes, width = ref.shape
    flat = ref.reshape(blocks * rows * planes, width)
    flat[pl.ds(block * rows * planes + plane, rows, stride=planes), :] = value


def padded(size):
    return -(-size // 16) * 16


def along_x(groups, matrix, emit):
    blocks, _, planes, width = groups[0][0].shape
    left_high, left_low = halves(matrix)
    left = jnp.concatenate([left_high, left_low], axis=0)
    left = jnp.concatenate([left, left], axis=1)

    def column(block, plane):
        parts = []
        for group in groups:
            parts += [x_plane(piece, block, plane) for piece in group]
            size = sum(piece.shape[1] for piece in group)
            if padded(size) > size:
                parts.append(jnp.zeros((padded(size) - size, width), jnp.float32))
        return jnp.concatenate(parts, axis=0)

    def pair(index, _):
        block, plane = index // (planes // 2), (index % (planes // 2)) * 2
        columns = jnp.concatenate([column(block, plane), column(block, plane + 1)], axis=1)
        product = jnp.dot(
            left, jnp.concatenate(halves(columns), axis=0), preferred_element_type=jnp.float32
        )
        mixed = product[: product.shape[0] // 2] + product[product.shape[0] // 2 :]
        emit(block, plane, mixed[:, :width])
        emit(block, plane + 1, mixed[:, width:])
        return 0

    lax.fori_loop(0, blocks * planes // 2, pair, 0, unroll=4)


def x_matrix(taps, groups, target):
    margin, nowhere = taps.shape[0] // 2, 1 << 20
    source = np.concatenate(
        [np.r_[np.arange(x, x + n), np.full(padded(n) - n, nowhere)] for x, n in groups]
    )
    rows = np.arange(padded(target[1]))
    offset = source[None, :] - (target[0] + rows)[:, None] + margin
    offset = np.where(rows[:, None] < target[1], offset, -1).astype(np.int32)
    stencil = jnp.arange(taps.shape[0], dtype=jnp.int32)
    picked = (jnp.asarray(offset)[None] == stencil[:, None, None]).astype(jnp.float32)
    return jnp.sum(taps[:, None, None] * picked, axis=0)


def plane_loader(ref):
    blocks, _, planes, width = ref.shape
    return lambda row: ref[:, row].reshape(blocks * planes, width)


def plane_storer(ref):
    blocks, _, planes, width = ref.shape

    def store(row, value):
        ref[:, row] = value.reshape(blocks, planes, width)

    return store


def copy_ends(first, second, head, tail):
    rows, kept = second.shape[1], head.shape[1]
    head[...] = first[:, :kept]
    tail[...] = second[:, rows - kept :]


def divide_yz(blurred, data, out, matrix_y, matrix_z, begin=0, place=0):
    data_of, blurred_of = plane_loader(data), plane_loader(blurred)
    along_yz(
        lambda row: data_of(place + row) / blurred_of(begin + row),
        plane_storer(out),
        matrix_y,
        matrix_z,
        out.shape[1],
    )


def blur(wide, mixed, blurred, blur_x, blur_y, blur_z):
    along_yz(plane_loader(wide), plane_storer(mixed), blur_y[...], blur_z[...], wide.shape[1])
    rows = blurred.shape[1]
    along_x([[mixed]], blur_x[...], lambda b, p, value: set_x_plane(blurred, b, p, value[:rows]))


def update(spread_x, above, center, below, before, wide):
    rows = wide.shape[1]

    def emit(block, plane, value):
        set_x_plane(wide, block, plane, x_plane(before, block, plane) * value[:rows])

    along_x([[above], [center], [below]], spread_x[...], emit)


def first_kernel(
    blur_x, blur_y, blur_z, back_y, back_z, above, own, below, data, wide, out, head, tail, mixed, blurred
):
    margin, rows = above.shape[1], own.shape[1]
    wide[:, :margin] = above[...]
    wide[:, margin : margin + rows] = own[...]
    wide[:, margin + rows : rows + 2 * margin] = below[...]
    if wide.shape[1] > rows + 2 * margin:
        wide[:, rows + 2 * margin :] = jnp.zeros_like(wide[:, rows + 2 * margin :])
    blur(wide, mixed, blurred, blur_x, blur_y, blur_z)
    divide_yz(blurred, data, out, back_y[...], back_z[...])
    copy_ends(out, out, head, tail)


def view_kernel(
    spread_x, blur_x, blur_y, blur_z, back_y, back_z, above, center, below, before, data,
    wide, out, head, tail, mixed, blurred,
):
    update(spread_x, above, center, below, before, wide)
    blur(wide, mixed, blurred, blur_x, blur_y, blur_z)
    divide_yz(blurred, data, out, back_y[...], back_z[...])
    copy_ends(out, out, head, tail)


def last_kernel(
    margin, spread_x, blur_x, blur_y, blur_z, back_y, back_z, above, center, below, before, data,
    own, inner, out_0, out_1, head, tail, wide, mixed, blurred,
):
    update(spread_x, above, center, below, before, wide)
    own[...] = wide[:, margin : margin + own.shape[1]]
    blur(wide, mixed, blurred, blur_x, blur_y, blur_z)
    outer, between = out_0.shape[1], inner.shape[1]
    inner[...] = blurred[:, outer : outer + between]
    divide_yz(blurred, data, out_0, back_y[...], back_z[...])
    divide_yz(blurred, data, out_1, back_y[...], back_z[...], outer + between, outer)
    copy_ends(out_0, out_1, head, tail)


def middle_kernel(back_y, back_z, blurred, data, out):
    divide_yz(blurred, data, out, back_y[...], back_z[...])


def finish_kernel(count, spread_x, above, below, current, *rest):
    pieces, updated = rest[:count], rest[count]
    rows = updated.shape[1]

    def emit(block, plane, value):
        set_x_plane(updated, block, plane, x_plane(current, block, plane) * value[:rows])

    along_x([[above], pieces, [below]], spread_x[...], emit)


def striped(kernel, name, microseconds, inputs, outs):
    blocks = outs[0].shape[0]
    step = 4 if blocks % 4 == 0 else 1

    def spec(array):
        return pl.BlockSpec((step,) + array.shape[1:], lambda g: (g, 0, 0, 0))

    return pl.pallas_call(
        kernel,
        grid=(blocks // step,),
        out_shape=outs,
        in_specs=[WHOLE] + [spec(array) for array in inputs[1:]],
        out_specs=[spec(array) for array in outs],
        compiler_params=pltpu.CompilerParams(vmem_limit_bytes=VMEM_LIMIT),
        cost_estimate=cost(microseconds),
        name=name,
    )(*inputs)


def call(kernel, name, microseconds, outs, in_specs, scratch=()):
    return pl.pallas_call(
        kernel,
        out_shape=outs,
        in_specs=in_specs,
        out_specs=jax.tree.map(lambda _: WHOLE, outs),
        scratch_shapes=list(scratch),
        compiler_params=pltpu.CompilerParams(vmem_limit_bytes=VMEM_LIMIT),
        cost_estimate=cost(microseconds),
        name=name,
    )


def source_block(place, run):
    return jnp.where(pl.program_id(0) % 2 == 0, place, run - 1 - place)


def turn_kernel(run, chosen, source, *rest):
    target = rest[-1]
    depth, extent, width = source.shape
    flat = source.reshape(depth * extent, width)
    for place in range(run):
        base = source_block(place, run) * (extent // run)
        for place_row, row in enumerate(chosen):
            target[place, place_row] = flat[pl.ds(base + row, depth, stride=extent), :]


def turn_back_kernel(run, source, target):
    _, rows, depth, width = source.shape
    flat = source.reshape(run * rows * depth, width)
    for place in range(run):
        base = source_block(place, run) * rows
        for plane in range(depth):
            for row in range(0, rows, 8):
                target[plane, pl.ds(pl.multiple_of(base + row, 8), 8), :] = flat[
                    pl.ds((place * rows + row) * depth + plane, 8, stride=depth), :
                ]


def gate(blocks, arrays):
    return pl.pallas_call(
        lambda *refs: None,
        out_shape=jax.ShapeDtypeStruct(blocks.shape, blocks.dtype),
        in_specs=[ANYWHERE] * (1 + len(arrays)),
        out_specs=ANYWHERE,
        input_output_aliases={0: 0},
        cost_estimate=cost(0.5),
        name="gate",
    )(blocks, *arrays)


def to_pencils(planes, count, run, chosen, turn_after=(), send_after=()):
    depth, extent, width = planes.shape
    rows = extent // count
    size = len(chosen)
    if depth % 8 == 0 and rows % 8 == 0:
        blocks = pl.pallas_call(
            functools.partial(turn_kernel, run, chosen),
            grid=(count // run,),
            out_shape=jax.ShapeDtypeStruct((count, size, depth, width), planes.dtype),
            in_specs=[pl.BlockSpec((depth, run * rows, width), lambda g: (0, g, 0))]
            + [ANYWHERE] * len(turn_after),
            out_specs=pl.BlockSpec((run, size, depth, width), lambda g: (g, 0, 0, 0)),
            compiler_params=pltpu.CompilerParams(vmem_limit_bytes=VMEM_LIMIT),
            cost_estimate=cost(TURN_US),
            name="turn",
        )(planes, *turn_after)
        if send_after:
            blocks = gate(blocks, send_after)
        return lax.all_to_all(blocks, "slab", split_axis=0, concat_axis=0, tiled=True)
    order = device_order(count, run)
    blocks = planes.reshape(depth, count, rows, width)[:, :, np.array(chosen)].transpose(1, 0, 2, 3)
    blocks = jnp.stack([blocks[order.index(d)] for d in range(count)])
    blocks = lax.all_to_all(blocks, "slab", split_axis=0, concat_axis=0, tiled=True)
    return blocks.reshape(1, count * depth, size, width).swapaxes(1, 2)


def to_planes(pencils, count, run, depth):
    rows, width = pencils.shape[1], pencils.shape[3]
    if depth % 8 == 0 and rows % 8 == 0:
        blocks = lax.all_to_all(pencils, "slab", split_axis=0, concat_axis=0, tiled=True)
        return pl.pallas_call(
            functools.partial(turn_back_kernel, run),
            grid=(count // run,),
            out_shape=jax.ShapeDtypeStruct((depth, rows * count, width), pencils.dtype),
            in_specs=[pl.BlockSpec((run, rows, depth, width), lambda g: (g, 0, 0, 0))],
            out_specs=pl.BlockSpec((depth, run * rows, width), lambda g: (0, g, 0)),
            compiler_params=pltpu.CompilerParams(vmem_limit_bytes=VMEM_LIMIT),
            cost_estimate=cost(TURN_US),
            name="turn_back",
        )(blocks)
    order = device_order(count, run)
    blocks = pencils.swapaxes(1, 2).reshape(count, depth, rows, width)
    blocks = lax.all_to_all(blocks, "slab", split_axis=0, concat_axis=0, tiled=True)
    blocks = jnp.stack([blocks[d] for d in order])
    return blocks.transpose(1, 0, 2, 3).reshape(depth, rows * count, width)


def halos(head, tail, margin, count, run):
    order = device_order(count, run)
    rows = head.shape[1]
    above, below, need, hop = [], [], margin, 1
    while need > 0:
        size = min(rows, need)
        forth = [(order[p], order[p + hop]) for p in range(count - hop)]
        back = [(order[p + hop], order[p]) for p in range(count - hop)]
        above.insert(0, lax.ppermute(tail[:, rows - size :], "slab", forth))
        below.append(lax.ppermute(head[:, :size], "slab", back))
        need, hop = need - size, hop + 1
    if len(above) == 1:
        return above[0], below[0]
    return jnp.concatenate(above, axis=1), jnp.concatenate(below, axis=1)


def body(estimate, recorded, lateral, axial_taps):
    count = lax.axis_size("slab")
    run = max(count // 4, 1)
    depth, rows, width = estimate.shape[0], estimate.shape[1] // count, estimate.shape[2]
    views, margin = recorded.shape[0], lateral.shape[2] // 2
    last = views - 1
    every = tuple(range(rows))

    current = to_pencils(estimate, count, run, every)
    data = to_pencils(recorded[0], count, run, every)
    blocks, _, planes, _ = current.shape

    def volume(size):
        return jax.ShapeDtypeStruct((blocks, size, planes, width), jnp.float32)

    def held(size):
        return pltpu.VMEM((blocks, size, planes, width), jnp.float32)

    extent, double = padded(rows + 2 * margin), 2 * margin
    end = volume(min(double, rows))
    taps = [normalized(lateral[v, 0]) for v in range(views)]
    columns = [banded(normalized(lateral[v, 1]), width) for v in range(views)]
    depths = [banded(normalized(axial_taps[v]), blocks * planes) for v in range(views)]
    blur_x = [x_matrix(t[::-1], [(-margin, extent)], (0, rows)) for t in taps]
    sides = [(-double, double), (0, rows), (rows, double)]
    spread_x = [x_matrix(t, sides, (-margin, rows + double)) for t in taps[:last]]
    sides = [(-margin, margin), (0, rows), (rows, margin)]
    finish_x = x_matrix(taps[last], sides, (0, rows))

    def matrices(v):
        return blur_x[v], columns[v], depths[v].T, columns[v].T, depths[v]

    outer = 9 * rows // 32
    split = outer >= margin + 1 and outer % 2 == 0 and views > 1
    ends = tuple(r for r in every if r < outer or r >= rows - outer)
    inside = tuple(r for r in every if outer <= r < rows - outer)

    above, below = halos(current[:, :margin], current[:, rows - margin :] if rows > margin else current, margin, count, run)
    for v in range(views):
        if v < last:
            chosen = ends if split and v + 1 == last else every
            order = (head,) if v else ()
            coming = to_pencils(recorded[v + 1], count, run, chosen, order, (above, below))
        if v == 0:
            wide, center, head, tail = call(
                first_kernel, "first", 26, (volume(extent), volume(rows), end, end), [WHOLE] * 9,
                [held(extent), held(rows)],
            )(*matrices(v), above, current, below, data)
        elif v == last and split:
            coming = to_pencils(recorded[v], count, run, inside, (head,), (above, below))
            outs = [volume(n) for n in (rows, rows - 2 * outer, outer, outer, margin, margin)]
            own, blurred, first, second, head, tail = call(
                functools.partial(last_kernel, margin), "last", 30, tuple(outs), [WHOLE] * 11,
                [held(extent), held(extent), held(rows)],
            )(spread_x[v - 1], *matrices(v), above, center, below, wide, data)
        else:
            wide, center, head, tail = call(
                view_kernel, "view", 33, (volume(extent), volume(rows), end, end), [WHOLE] * 11,
                [held(extent), held(rows)],
            )(spread_x[v - 1], *matrices(v), above, center, below, wide, data)
        reach = double
        if v == last:
            reach = margin
            head, tail = head[:, :margin], tail[:, max(tail.shape[1] - margin, 0) :]
        above, below = halos(head, tail, reach, count, run)
        data = coming
    if split:
        inner = call(middle_kernel, "middle", 3, volume(rows - 2 * outer), [WHOLE] * 4)(
            columns[last].T, depths[last], blurred, data
        )
        pieces = [first, inner, second]
    else:
        own, pieces = wide[:, margin : margin + rows], [center]
    (current,) = striped(
        functools.partial(finish_kernel, len(pieces)),
        "finish",
        8,
        [finish_x, above, below, own, *pieces],
        [volume(rows)],
    )
    return to_planes(current, count, run, depth)


def solution(mesh):
    in_specs = (P("slab", "groups", None), P(None, "slab", "groups", None), P(), P())
    out_specs = P("slab", "groups", None)
    return jax.shard_map(body, mesh=mesh, in_specs=in_specs, out_specs=out_specs, check_vma=False)
```

```python
import functools

import jax
import jax.numpy as jnp
import numpy as np
from jax import lax
from jax.experimental import pallas as pl
from jax.experimental.pallas import tpu as pltpu
from jax.sharding import PartitionSpec as P

VMEM_LIMIT = 56 * 1024 * 1024
WHOLE = pl.BlockSpec(memory_space=pltpu.VMEM)
ANYWHERE = pl.BlockSpec(memory_space=pl.ANY)
TURN_US = 4


def cost(microseconds):
    return pl.CostEstimate(flops=0, bytes_accessed=int(microseconds * 3.6e6), transcendentals=0)


def banded(kernel, extent):
    length = kernel.shape[0]
    margin = length // 2
    places = jnp.arange(extent, dtype=jnp.int32)
    offsets = places[None, :] - places[:, None] + margin
    stencil = jnp.arange(length, dtype=jnp.int32)
    picked = (offsets[None, :, :] == stencil[:, None, None]).astype(jnp.float32)
    return jnp.sum(kernel[:, None, None] * picked, axis=0)


def normalized(kernel):
    return kernel / jnp.sum(kernel)


def halves(value):
    high = value.astype(jnp.bfloat16)
    low = (value - high.astype(jnp.float32)).astype(jnp.bfloat16)
    return high, low


def position(device, run):
    row, place = device // run, device % run
    return row * run + jnp.where(row % 2 == 0, place, run - 1 - place)


def device_order(count, run):
    return [r * run + (p if r % 2 == 0 else run - 1 - p) for r in range(count // run) for p in range(run)]


def along_yz(load, store, matrix_y, matrix_z, rows):
    depth, width = matrix_z.shape[0], matrix_y.shape[0]
    right_high, right_low = halves(matrix_y)
    right = jnp.concatenate([right_high, right_low], axis=1)
    right = jnp.concatenate([right, right], axis=0)
    left_high, left_low = halves(matrix_z)
    left = jnp.concatenate([left_high, left_low], axis=0)
    left = jnp.concatenate([left, left], axis=1)

    def pair(index, _):
        row = 2 * index
        planes = jnp.concatenate([load(row), load(row + 1)], axis=0)
        product = jnp.dot(
            jnp.concatenate(halves(planes), axis=1), right, preferred_element_type=jnp.float32
        )
        mixed = product[:, :width] + product[:, width:]
        sides = jnp.concatenate([mixed[:depth], mixed[depth:]], axis=1)
        product = jnp.dot(
            left, jnp.concatenate(halves(sides), axis=0), preferred_element_type=jnp.float32
        )
        mixed = product[:depth] + product[depth:]
        store(row, mixed[:, :width])
        store(row + 1, mixed[:, width:])
        return 0

    lax.fori_loop(0, rows // 2, pair, 0, unroll=4)


def x_plane(ref, block, plane):
    blocks, rows, planes, width = ref.shape
    flat = ref.reshape(blocks * rows * planes, width)
    return flat[pl.ds(block * rows * planes + plane, rows, stride=planes), :]


def set_x_plane(ref, block, plane, value):
    blocks, rows, planes, width = ref.shape
    flat = ref.reshape(blocks * rows * planes, width)
    flat[pl.ds(block * rows * planes + plane, rows, stride=planes), :] = value


def padded(size):
    return -(-size // 16) * 16


def along_x(groups, matrix, emit, first=0, blocks=None):
    _, _, planes, width = groups[0][0].shape
    blocks = groups[0][0].shape[0] if blocks is None else blocks
    left_high, left_low = halves(matrix)
    left = jnp.concatenate([left_high, left_low], axis=0)
    left = jnp.concatenate([left, left], axis=1)

    def column(block, plane):
        parts = []
        for group in groups:
            parts += [x_plane(piece, block, plane) for piece in group]
            size = sum(piece.shape[1] for piece in group)
            if padded(size) > size:
                parts.append(jnp.zeros((padded(size) - size, width), jnp.float32))
        return jnp.concatenate(parts, axis=0)

    def pair(index, _):
        block, plane = first + index // (planes // 2), (index % (planes // 2)) * 2
        columns = jnp.concatenate([column(block, plane), column(block, plane + 1)], axis=1)
        product = jnp.dot(
            left, jnp.concatenate(halves(columns), axis=0), preferred_element_type=jnp.float32
        )
        mixed = product[: product.shape[0] // 2] + product[product.shape[0] // 2 :]
        emit(block, plane, mixed[:, :width])
        emit(block, plane + 1, mixed[:, width:])
        return 0

    lax.fori_loop(0, blocks * planes // 2, pair, 0, unroll=4)


def x_matrix(taps, groups, target):
    margin, nowhere = taps.shape[0] // 2, 1 << 20
    source = np.concatenate(
        [np.r_[np.arange(x, x + n), np.full(padded(n) - n, nowhere)] for x, n in groups]
    )
    rows = np.arange(padded(target[1]))
    offset = source[None, :] - (target[0] + rows)[:, None] + margin
    offset = np.where(rows[:, None] < target[1], offset, -1).astype(np.int32)
    stencil = jnp.arange(taps.shape[0], dtype=jnp.int32)
    picked = (jnp.asarray(offset)[None] == stencil[:, None, None]).astype(jnp.float32)
    return jnp.sum(taps[:, None, None] * picked, axis=0)


def plane_loader(ref):
    blocks, _, planes, width = ref.shape
    return lambda row: ref[:, row].reshape(blocks * planes, width)


def plane_storer(ref):
    blocks, _, planes, width = ref.shape

    def store(row, value):
        ref[:, row] = value.reshape(blocks, planes, width)

    return store


def copy_ends(first, second, head, tail):
    rows, kept = second.shape[1], head.shape[1]
    head[...] = first[:, :kept]
    tail[...] = second[:, rows - kept :]


def divide_yz(blurred, data, out, matrix_y, matrix_z, begin=0, place=0):
    data_of, blurred_of = plane_loader(data), plane_loader(blurred)
    along_yz(
        lambda row: data_of(place + row) / blurred_of(begin + row),
        plane_storer(out),
        matrix_y,
        matrix_z,
        out.shape[1],
    )


def blur(wide, mixed, blurred, blur_x, blur_y, blur_z):
    along_yz(plane_loader(wide), plane_storer(mixed), blur_y[...], blur_z[...], wide.shape[1])
    rows = blurred.shape[1]
    along_x([[mixed]], blur_x[...], lambda b, p, value: set_x_plane(blurred, b, p, value[:rows]))


def update(spread_x, above, center, below, before, wide):
    rows = wide.shape[1]

    def emit(block, plane, value):
        set_x_plane(wide, block, plane, x_plane(before, block, plane) * value[:rows])

    along_x([[above], [center], [below]], spread_x[...], emit)


def first_kernel(
    blur_x, blur_y, blur_z, back_y, back_z, above, own, below, data, wide, out, head, tail, mixed, blurred
):
    margin, rows = above.shape[1], own.shape[1]
    wide[:, :margin] = above[...]
    wide[:, margin : margin + rows] = own[...]
    wide[:, margin + rows : rows + 2 * margin] = below[...]
    if wide.shape[1] > rows + 2 * margin:
        wide[:, rows + 2 * margin :] = jnp.zeros_like(wide[:, rows + 2 * margin :])
    blur(wide, mixed, blurred, blur_x, blur_y, blur_z)
    divide_yz(blurred, data, out, back_y[...], back_z[...])
    copy_ends(out, out, head, tail)


def view_kernel(
    spread_x, blur_x, blur_y, blur_z, back_y, back_z, above, center, below, before, data,
    wide, out, head, tail, mixed, blurred,
):
    update(spread_x, above, center, below, before, wide)
    blur(wide, mixed, blurred, blur_x, blur_y, blur_z)
    divide_yz(blurred, data, out, back_y[...], back_z[...])
    copy_ends(out, out, head, tail)


def last_kernel(
    margin, spread_x, blur_x, blur_y, blur_z, back_y, back_z, above, center, below, before, data,
    own, inner, out_0, out_1, head, tail, wide, mixed, blurred,
):
    update(spread_x, above, center, below, before, wide)
    own[...] = wide[:, margin : margin + own.shape[1]]
    blur(wide, mixed, blurred, blur_x, blur_y, blur_z)
    outer, between = out_0.shape[1], inner.shape[1]
    inner[...] = blurred[:, outer : outer + between]
    divide_yz(blurred, data, out_0, back_y[...], back_z[...])
    divide_yz(blurred, data, out_1, back_y[...], back_z[...], outer + between, outer)
    copy_ends(out_0, out_1, head, tail)


def middle_kernel(back_y, back_z, blurred, data, out):
    divide_yz(blurred, data, out, back_y[...], back_z[...])


def finish_part(blocks, step, fixed, sources, targets):
    (spread_x,), (above, below, current, *pieces), (updated,) = fixed, sources, targets
    rows = updated.shape[1]

    def emit(block, plane, value):
        set_x_plane(updated, block, plane, x_plane(current, block, plane) * value[:rows])

    along_x([[above], pieces, [below]], spread_x[...], emit, step * blocks, blocks)


def streamed(part, name, microseconds, steps, fixed, inputs, outs, cuts, after=(), spare=0):
    counts = len(fixed), len(inputs), len(after), len(outs), len(inputs), len(outs)

    def kernel(*refs):
        groups, start = [], 0
        for size in counts:
            groups.append(refs[start : start + size])
            start += size
        held, sources, _, targets, ins, ready = groups
        in_sem, out_sem = refs[start:]

        def come(k, step):
            cut = cuts[0](step)
            return pltpu.make_async_copy(sources[k].at[cut], ins[k].at[cut], in_sem.at[k, step])

        def go(k, step):
            cut = cuts[1](step)
            return pltpu.make_async_copy(ready[k].at[cut], targets[k].at[cut], out_sem.at[k, step])

        def begin(step, _):
            for k in range(len(inputs)):
                come(k, step).start()
            return 0

        def work(step, _):
            for k in range(len(inputs)):
                come(k, step).wait()
            part(step, held, ins, ready)
            for k in range(len(outs)):
                go(k, step).start()
            return 0

        def end(step, _):
            for k in range(len(outs)):
                go(k, step).wait()
            return 0

        lax.fori_loop(0, steps, begin, 0)
        lax.fori_loop(0, steps, work, 0)
        lax.fori_loop(0, steps, end, 0)

    def scratch(array, more):
        shape = array.shape if len(array.shape) == 4 else (array.shape[0], array.shape[1] + more, array.shape[2])
        return pltpu.VMEM(shape, jnp.float32)

    return pl.pallas_call(
        kernel,
        out_shape=outs,
        in_specs=[WHOLE] * len(fixed) + [ANYWHERE] * (len(inputs) + len(after)),
        out_specs=[ANYWHERE] * len(outs),
        scratch_shapes=[scratch(array, spare) for array in inputs]
        + [scratch(array, 0) for array in outs]
        + [pltpu.SemaphoreType.DMA((len(inputs), steps)), pltpu.SemaphoreType.DMA((len(outs), steps))],
        compiler_params=pltpu.CompilerParams(vmem_limit_bytes=VMEM_LIMIT),
        cost_estimate=cost(microseconds),
        name=name,
    )(*fixed, *inputs, *after)


def call(kernel, name, microseconds, outs, in_specs, scratch=()):
    return pl.pallas_call(
        kernel,
        out_shape=outs,
        in_specs=in_specs,
        out_specs=jax.tree.map(lambda _: WHOLE, outs),
        scratch_shapes=list(scratch),
        compiler_params=pltpu.CompilerParams(vmem_limit_bytes=VMEM_LIMIT),
        cost_estimate=cost(microseconds),
        name=name,
    )


def x_rows(device, run, rows):
    return pl.ds(pl.multiple_of(position(device, run) * rows, 8), rows)


def turn_part(run, rows, chosen, device, _, sources, targets):
    (source,), (target,) = sources, targets
    depth, extent, width = source.shape
    flat = source.reshape(depth * extent, width)
    base = position(device, run) * rows
    for place, row in enumerate(chosen):
        target[device, place] = flat[pl.ds(base + row, depth, stride=extent), :]


def turn_back_part(run, device, _, sources, targets):
    (source,), (target,) = sources, targets
    count, rows, depth, width = source.shape
    flat = source.reshape(count * rows * depth, width)
    base = position(device, run) * rows
    for plane in range(depth):
        for row in range(0, rows, 8):
            target[plane, pl.ds(pl.multiple_of(base + row, 8), 8), :] = flat[
                pl.ds((device * rows + row) * depth + plane, 8, stride=depth), :
            ]


def gate(blocks, arrays):
    return pl.pallas_call(
        lambda *refs: None,
        out_shape=jax.ShapeDtypeStruct(blocks.shape, blocks.dtype),
        in_specs=[ANYWHERE] * (1 + len(arrays)),
        out_specs=ANYWHERE,
        input_output_aliases={0: 0},
        cost_estimate=cost(0.5),
        name="gate",
    )(blocks, *arrays)


def to_pencils(planes, count, run, chosen, turn_after=(), send_after=()):
    depth, extent, width = planes.shape
    rows = extent // count
    size = len(chosen)
    if depth % 8 == 0 and rows % 8 == 0:
        (blocks,) = streamed(
            functools.partial(turn_part, run, rows, chosen),
            "turn",
            TURN_US,
            count,
            [],
            [planes],
            [jax.ShapeDtypeStruct((count, size, depth, width), planes.dtype)],
            (lambda step: (slice(None), x_rows(step, run, rows)), lambda step: (pl.ds(step, 1),)),
            turn_after,
            8,
        )
        if send_after:
            blocks = gate(blocks, send_after)
        return lax.all_to_all(blocks, "slab", split_axis=0, concat_axis=0, tiled=True)
    order = device_order(count, run)
    blocks = planes.reshape(depth, count, rows, width)[:, :, np.array(chosen)].transpose(1, 0, 2, 3)
    blocks = jnp.stack([blocks[order.index(d)] for d in range(count)])
    blocks = lax.all_to_all(blocks, "slab", split_axis=0, concat_axis=0, tiled=True)
    return blocks.reshape(1, count * depth, size, width).swapaxes(1, 2)


def to_planes(pencils, count, run, depth):
    rows, width = pencils.shape[1], pencils.shape[3]
    if depth % 8 == 0 and rows % 8 == 0:
        blocks = lax.all_to_all(pencils, "slab", split_axis=0, concat_axis=0, tiled=True)
        return streamed(
            functools.partial(turn_back_part, run),
            "turn_back",
            TURN_US,
            count,
            [],
            [blocks],
            [jax.ShapeDtypeStruct((depth, rows * count, width), pencils.dtype)],
            (lambda step: (pl.ds(step, 1),), lambda step: (slice(None), x_rows(step, run, rows))),
        )[0]
    order = device_order(count, run)
    blocks = pencils.swapaxes(1, 2).reshape(count, depth, rows, width)
    blocks = lax.all_to_all(blocks, "slab", split_axis=0, concat_axis=0, tiled=True)
    blocks = jnp.stack([blocks[d] for d in order])
    return blocks.transpose(1, 0, 2, 3).reshape(depth, rows * count, width)


def halos(head, tail, margin, count, run):
    order = device_order(count, run)
    rows = head.shape[1]
    above, below, need, hop = [], [], margin, 1
    while need > 0:
        size = min(rows, need)
        forth = [(order[p], order[p + hop]) for p in range(count - hop)]
        back = [(order[p + hop], order[p]) for p in range(count - hop)]
        above.insert(0, lax.ppermute(tail[:, rows - size :], "slab", forth))
        below.append(lax.ppermute(head[:, :size], "slab", back))
        need, hop = need - size, hop + 1
    if len(above) == 1:
        return above[0], below[0]
    return jnp.concatenate(above, axis=1), jnp.concatenate(below, axis=1)


def body(estimate, recorded, lateral, axial_taps):
    count = lax.axis_size("slab")
    run = max(count // 4, 1)
    depth, rows, width = estimate.shape[0], estimate.shape[1] // count, estimate.shape[2]
    views, margin = recorded.shape[0], lateral.shape[2] // 2
    last = views - 1
    every = tuple(range(rows))

    current = to_pencils(estimate, count, run, every)
    data = to_pencils(recorded[0], count, run, every)
    blocks, _, planes, _ = current.shape

    def volume(size):
        return jax.ShapeDtypeStruct((blocks, size, planes, width), jnp.float32)

    def held(size):
        return pltpu.VMEM((blocks, size, planes, width), jnp.float32)

    extent, double = padded(rows + 2 * margin), 2 * margin
    end = volume(min(double, rows))
    taps = [normalized(lateral[v, 0]) for v in range(views)]
    columns = [banded(normalized(lateral[v, 1]), width) for v in range(views)]
    depths = [banded(normalized(axial_taps[v]), blocks * planes) for v in range(views)]
    blur_x = [x_matrix(t[::-1], [(-margin, extent)], (0, rows)) for t in taps]
    sides = [(-double, double), (0, rows), (rows, double)]
    spread_x = [x_matrix(t, sides, (-margin, rows + double)) for t in taps[:last]]
    sides = [(-margin, margin), (0, rows), (rows, margin)]
    finish_x = x_matrix(taps[last], sides, (0, rows))

    def matrices(v):
        return blur_x[v], columns[v], depths[v].T, columns[v].T, depths[v]

    outer = 9 * rows // 32
    split = outer >= margin + 1 and outer % 2 == 0 and views > 1
    ends = tuple(r for r in every if r < outer or r >= rows - outer)
    inside = tuple(r for r in every if outer <= r < rows - outer)

    above, below = halos(current[:, :margin], current[:, rows - margin :] if rows > margin else current, margin, count, run)
    for v in range(views):
        if v < last:
            chosen = ends if split and v + 1 == last else every
            order = (head,) if v else ()
            coming = to_pencils(recorded[v + 1], count, run, chosen, order, (above, below))
        if v == 0:
            wide, center, head, tail = call(
                first_kernel, "first", 26, (volume(extent), volume(rows), end, end), [WHOLE] * 9,
                [held(extent), held(rows)],
            )(*matrices(v), above, current, below, data)
        elif v == last and split:
            coming = to_pencils(recorded[v], count, run, inside, (head,), (above, below))
            outs = [volume(n) for n in (rows, rows - 2 * outer, outer, outer, margin, margin)]
            own, blurred, first, second, head, tail = call(
                functools.partial(last_kernel, margin), "last", 30, tuple(outs), [WHOLE] * 11,
                [held(extent), held(extent), held(rows)],
            )(spread_x[v - 1], *matrices(v), above, center, below, wide, data)
        else:
            wide, center, head, tail = call(
                view_kernel, "view", 33, (volume(extent), volume(rows), end, end), [WHOLE] * 11,
                [held(extent), held(rows)],
            )(spread_x[v - 1], *matrices(v), above, center, below, wide, data)
        reach = double
        if v == last:
            reach = margin
            head, tail = head[:, :margin], tail[:, max(tail.shape[1] - margin, 0) :]
        above, below = halos(head, tail, reach, count, run)
        data = coming
    if split:
        inner = call(middle_kernel, "middle", 3, volume(rows - 2 * outer), [WHOLE] * 4)(
            columns[last].T, depths[last], blurred, data
        )
        pieces = [first, inner, second]
    else:
        own, pieces = wide[:, margin : margin + rows], [center]
    step = 2 if blocks % 2 == 0 else 1
    cut = lambda place: (pl.ds(place * step, step),)
    (current,) = streamed(
        functools.partial(finish_part, step),
        "finish",
        7,
        blocks // step,
        [finish_x],
        [above, below, own, *pieces],
        [volume(rows)],
        (cut, cut),
    )
    return to_planes(current, count, run, depth)


def solution(mesh):
    in_specs = (P("slab", "groups", None), P(None, "slab", "groups", None), P(), P())
    out_specs = P("slab", "groups", None)
    return jax.shard_map(body, mesh=mesh, in_specs=in_specs, out_specs=out_specs, check_vma=False)
```

```python
import functools

import jax
import jax.numpy as jnp
import numpy as np
from jax import lax
from jax.experimental import pallas as pl
from jax.experimental.pallas import tpu as pltpu
from jax.sharding import PartitionSpec as P

VMEM_LIMIT = 56 * 1024 * 1024
WHOLE = pl.BlockSpec(memory_space=pltpu.VMEM)
ANYWHERE = pl.BlockSpec(memory_space=pl.ANY)
TURN_US = 4


def cost(microseconds):
    return pl.CostEstimate(flops=0, bytes_accessed=int(microseconds * 3.6e6), transcendentals=0)


def banded(kernel, extent):
    length = kernel.shape[0]
    margin = length // 2
    places = jnp.arange(extent, dtype=jnp.int32)
    offsets = places[None, :] - places[:, None] + margin
    stencil = jnp.arange(length, dtype=jnp.int32)
    picked = (offsets[None, :, :] == stencil[:, None, None]).astype(jnp.float32)
    return jnp.sum(kernel[:, None, None] * picked, axis=0)


def normalized(kernel):
    return kernel / jnp.sum(kernel)


def halves(value):
    high = value.astype(jnp.bfloat16)
    low = (value - high.astype(jnp.float32)).astype(jnp.bfloat16)
    return high, low


def position(device, run):
    row, place = device // run, device % run
    return row * run + jnp.where(row % 2 == 0, place, run - 1 - place)


def device_order(count, run):
    return [r * run + (p if r % 2 == 0 else run - 1 - p) for r in range(count // run) for p in range(run)]


def along_yz(load, store, matrix_y, matrix_z, rows):
    depth, width = matrix_z.shape[0], matrix_y.shape[0]
    right_high, right_low = halves(matrix_y)
    right = jnp.concatenate([right_high, right_low], axis=1)
    right = jnp.concatenate([right, right], axis=0)
    left_high, left_low = halves(matrix_z)
    left = jnp.concatenate([left_high, left_low], axis=0)
    left = jnp.concatenate([left, left], axis=1)

    def pair(index, _):
        row = 2 * index
        planes = jnp.concatenate([load(row), load(row + 1)], axis=0)
        product = jnp.dot(
            jnp.concatenate(halves(planes), axis=1), right, preferred_element_type=jnp.float32
        )
        mixed = product[:, :width] + product[:, width:]
        sides = jnp.concatenate([mixed[:depth], mixed[depth:]], axis=1)
        product = jnp.dot(
            left, jnp.concatenate(halves(sides), axis=0), preferred_element_type=jnp.float32
        )
        mixed = product[:depth] + product[depth:]
        store(row, mixed[:, :width])
        store(row + 1, mixed[:, width:])
        return 0

    lax.fori_loop(0, rows // 2, pair, 0, unroll=4)


def x_plane(ref, block, plane):
    blocks, rows, planes, width = ref.shape
    flat = ref.reshape(blocks * rows * planes, width)
    return flat[pl.ds(block * rows * planes + plane, rows, stride=planes), :]


def set_x_plane(ref, block, plane, value):
    blocks, rows, planes, width = ref.shape
    flat = ref.reshape(blocks * rows * planes, width)
    flat[pl.ds(block * rows * planes + plane, rows, stride=planes), :] = value


def padded(size):
    return -(-size // 16) * 16


def along_x(groups, matrix, emit, first=0, blocks=None):
    _, _, planes, width = groups[0][0].shape
    blocks = groups[0][0].shape[0] if blocks is None else blocks
    left_high, left_low = halves(matrix)
    left = jnp.concatenate([left_high, left_low], axis=0)
    left = jnp.concatenate([left, left], axis=1)

    def column(block, plane):
        parts = []
        for group in groups:
            parts += [x_plane(piece, block, plane) for piece in group]
            size = sum(piece.shape[1] for piece in group)
            if padded(size) > size:
                parts.append(jnp.zeros((padded(size) - size, width), jnp.float32))
        return jnp.concatenate(parts, axis=0)

    def pair(index, _):
        block, plane = first + index // (planes // 2), (index % (planes // 2)) * 2
        columns = jnp.concatenate([column(block, plane), column(block, plane + 1)], axis=1)
        product = jnp.dot(
            left, jnp.concatenate(halves(columns), axis=0), preferred_element_type=jnp.float32
        )
        mixed = product[: product.shape[0] // 2] + product[product.shape[0] // 2 :]
        emit(block, plane, mixed[:, :width])
        emit(block, plane + 1, mixed[:, width:])
        return 0

    lax.fori_loop(0, blocks * planes // 2, pair, 0, unroll=8)


def x_matrix(taps, groups, target):
    margin, nowhere = taps.shape[0] // 2, 1 << 20
    source = np.concatenate(
        [np.r_[np.arange(x, x + n), np.full(padded(n) - n, nowhere)] for x, n in groups]
    )
    rows = np.arange(padded(target[1]))
    offset = source[None, :] - (target[0] + rows)[:, None] + margin
    offset = np.where(rows[:, None] < target[1], offset, -1).astype(np.int32)
    stencil = jnp.arange(taps.shape[0], dtype=jnp.int32)
    picked = (jnp.asarray(offset)[None] == stencil[:, None, None]).astype(jnp.float32)
    return jnp.sum(taps[:, None, None] * picked, axis=0)


def plane_loader(ref):
    blocks, _, planes, width = ref.shape
    return lambda row: ref[:, row].reshape(blocks * planes, width)


def plane_storer(ref):
    blocks, _, planes, width = ref.shape

    def store(row, value):
        ref[:, row] = value.reshape(blocks, planes, width)

    return store


def copy_ends(first, second, head, tail):
    rows, kept = second.shape[1], head.shape[1]
    head[...] = first[:, :kept]
    tail[...] = second[:, rows - kept :]


def divide_yz(blurred, data, out, matrix_y, matrix_z, begin=0, place=0):
    data_of, blurred_of = plane_loader(data), plane_loader(blurred)
    along_yz(
        lambda row: data_of(place + row) / blurred_of(begin + row),
        plane_storer(out),
        matrix_y,
        matrix_z,
        out.shape[1],
    )


def blur(wide, mixed, blurred, blur_x, blur_y, blur_z):
    along_yz(plane_loader(wide), plane_storer(mixed), blur_y[...], blur_z[...], wide.shape[1])
    rows = blurred.shape[1]
    along_x([[mixed]], blur_x[...], lambda b, p, value: set_x_plane(blurred, b, p, value[:rows]))


def update(spread_x, above, center, below, before, wide):
    rows = wide.shape[1]

    def emit(block, plane, value):
        set_x_plane(wide, block, plane, x_plane(before, block, plane) * value[:rows])

    along_x([[above], [center], [below]], spread_x[...], emit)


def first_kernel(
    blur_x, blur_y, blur_z, back_y, back_z, above, own, below, data, wide, out, head, tail, mixed, blurred
):
    margin, rows = above.shape[1], own.shape[1]
    wide[:, :margin] = above[...]
    wide[:, margin : margin + rows] = own[...]
    wide[:, margin + rows : rows + 2 * margin] = below[...]
    if wide.shape[1] > rows + 2 * margin:
        wide[:, rows + 2 * margin :] = jnp.zeros_like(wide[:, rows + 2 * margin :])
    blur(wide, mixed, blurred, blur_x, blur_y, blur_z)
    divide_yz(blurred, data, out, back_y[...], back_z[...])
    copy_ends(out, out, head, tail)


def view_kernel(
    spread_x, blur_x, blur_y, blur_z, back_y, back_z, above, center, below, before, data,
    wide, out, head, tail, mixed, blurred,
):
    update(spread_x, above, center, below, before, wide)
    blur(wide, mixed, blurred, blur_x, blur_y, blur_z)
    divide_yz(blurred, data, out, back_y[...], back_z[...])
    copy_ends(out, out, head, tail)


def last_kernel(
    margin, spread_x, blur_x, blur_y, blur_z, back_y, back_z, above, center, below, before, data,
    own, inner, out_0, out_1, head, tail, wide, mixed, blurred,
):
    update(spread_x, above, center, below, before, wide)
    own[...] = wide[:, margin : margin + own.shape[1]]
    blur(wide, mixed, blurred, blur_x, blur_y, blur_z)
    outer, between = out_0.shape[1], inner.shape[1]
    inner[...] = blurred[:, outer : outer + between]
    divide_yz(blurred, data, out_0, back_y[...], back_z[...])
    divide_yz(blurred, data, out_1, back_y[...], back_z[...], outer + between, outer)
    copy_ends(out_0, out_1, head, tail)


def middle_kernel(back_y, back_z, blurred, data, out):
    divide_yz(blurred, data, out, back_y[...], back_z[...])


def finish_part(blocks, step, fixed, sources, targets):
    (spread_x,), (above, below, current, *pieces), (updated,) = fixed, sources, targets
    rows = updated.shape[1]

    def emit(block, plane, value):
        set_x_plane(updated, block, plane, x_plane(current, block, plane) * value[:rows])

    along_x([[above], pieces, [below]], spread_x[...], emit, step * blocks, blocks)


def streamed(part, name, microseconds, steps, fixed, inputs, outs, cuts, after=(), spare=0):
    counts = len(fixed), len(inputs), len(after), len(outs), len(inputs), len(outs)

    def kernel(*refs):
        groups, start = [], 0
        for size in counts:
            groups.append(refs[start : start + size])
            start += size
        held, sources, _, targets, ins, ready = groups
        in_sem, out_sem = refs[start:]

        def come(k, step):
            cut = cuts[0](step)
            return pltpu.make_async_copy(sources[k].at[cut], ins[k].at[cut], in_sem.at[k, step])

        def go(k, step):
            cut = cuts[1](step)
            return pltpu.make_async_copy(ready[k].at[cut], targets[k].at[cut], out_sem.at[k, step])

        def begin(step, _):
            for k in range(len(inputs)):
                come(k, step).start()
            return 0

        def work(step, _):
            for k in range(len(inputs)):
                come(k, step).wait()
            part(step, held, ins, ready)
            for k in range(len(outs)):
                go(k, step).start()
            return 0

        def end(step, _):
            for k in range(len(outs)):
                go(k, step).wait()
            return 0

        lax.fori_loop(0, steps, begin, 0)
        lax.fori_loop(0, steps, work, 0)
        lax.fori_loop(0, steps, end, 0)

    def scratch(array, more):
        shape = array.shape if len(array.shape) == 4 else (array.shape[0], array.shape[1] + more, array.shape[2])
        return pltpu.VMEM(shape, jnp.float32)

    return pl.pallas_call(
        kernel,
        out_shape=outs,
        in_specs=[WHOLE] * len(fixed) + [ANYWHERE] * (len(inputs) + len(after)),
        out_specs=[ANYWHERE] * len(outs),
        scratch_shapes=[scratch(array, spare) for array in inputs]
        + [scratch(array, 0) for array in outs]
        + [pltpu.SemaphoreType.DMA((len(inputs), steps)), pltpu.SemaphoreType.DMA((len(outs), steps))],
        compiler_params=pltpu.CompilerParams(vmem_limit_bytes=VMEM_LIMIT),
        cost_estimate=cost(microseconds),
        name=name,
    )(*fixed, *inputs, *after)


def call(kernel, name, microseconds, outs, in_specs, scratch=()):
    return pl.pallas_call(
        kernel,
        out_shape=outs,
        in_specs=in_specs,
        out_specs=jax.tree.map(lambda _: WHOLE, outs),
        scratch_shapes=list(scratch),
        compiler_params=pltpu.CompilerParams(vmem_limit_bytes=VMEM_LIMIT),
        cost_estimate=cost(microseconds),
        name=name,
    )


def x_rows(device, run, rows):
    return pl.ds(pl.multiple_of(position(device, run) * rows, 8), rows)


def turn_part(run, rows, chosen, device, _, sources, targets):
    (source,), (target,) = sources, targets
    depth, extent, width = source.shape
    flat = source.reshape(depth * extent, width)
    base = position(device, run) * rows
    for place, row in enumerate(chosen):
        target[device, place] = flat[pl.ds(base + row, depth, stride=extent), :]


def turn_back_part(run, device, _, sources, targets):
    (source,), (target,) = sources, targets
    count, rows, depth, width = source.shape
    flat = source.reshape(count * rows * depth, width)
    base = position(device, run) * rows
    for plane in range(depth):
        for row in range(0, rows, 8):
            target[plane, pl.ds(pl.multiple_of(base + row, 8), 8), :] = flat[
                pl.ds((device * rows + row) * depth + plane, 8, stride=depth), :
            ]


def gate(blocks, arrays):
    return pl.pallas_call(
        lambda *refs: None,
        out_shape=jax.ShapeDtypeStruct(blocks.shape, blocks.dtype),
        in_specs=[ANYWHERE] * (1 + len(arrays)),
        out_specs=ANYWHERE,
        input_output_aliases={0: 0},
        cost_estimate=cost(0.5),
        name="gate",
    )(blocks, *arrays)


def to_pencils(planes, count, run, chosen, turn_after=(), send_after=()):
    depth, extent, width = planes.shape
    rows = extent // count
    size = len(chosen)
    if depth % 8 == 0 and rows % 8 == 0:
        (blocks,) = streamed(
            functools.partial(turn_part, run, rows, chosen),
            "turn",
            TURN_US,
            count,
            [],
            [planes],
            [jax.ShapeDtypeStruct((count, size, depth, width), planes.dtype)],
            (lambda step: (slice(None), x_rows(step, run, rows)), lambda step: (pl.ds(step, 1),)),
            turn_after,
            8,
        )
        if send_after:
            blocks = gate(blocks, send_after)
        return lax.all_to_all(blocks, "slab", split_axis=0, concat_axis=0, tiled=True)
    order = device_order(count, run)
    blocks = planes.reshape(depth, count, rows, width)[:, :, np.array(chosen)].transpose(1, 0, 2, 3)
    blocks = jnp.stack([blocks[order.index(d)] for d in range(count)])
    blocks = lax.all_to_all(blocks, "slab", split_axis=0, concat_axis=0, tiled=True)
    return blocks.reshape(1, count * depth, size, width).swapaxes(1, 2)


def to_planes(pencils, count, run, depth):
    rows, width = pencils.shape[1], pencils.shape[3]
    if depth % 8 == 0 and rows % 8 == 0:
        blocks = lax.all_to_all(pencils, "slab", split_axis=0, concat_axis=0, tiled=True)
        return streamed(
            functools.partial(turn_back_part, run),
            "turn_back",
            TURN_US,
            count,
            [],
            [blocks],
            [jax.ShapeDtypeStruct((depth, rows * count, width), pencils.dtype)],
            (lambda step: (pl.ds(step, 1),), lambda step: (slice(None), x_rows(step, run, rows))),
        )[0]
    order = device_order(count, run)
    blocks = pencils.swapaxes(1, 2).reshape(count, depth, rows, width)
    blocks = lax.all_to_all(blocks, "slab", split_axis=0, concat_axis=0, tiled=True)
    blocks = jnp.stack([blocks[d] for d in order])
    return blocks.transpose(1, 0, 2, 3).reshape(depth, rows * count, width)


def halos(head, tail, margin, count, run):
    order = device_order(count, run)
    rows = head.shape[1]
    above, below, need, hop = [], [], margin, 1
    while need > 0:
        size = min(rows, need)
        forth = [(order[p], order[p + hop]) for p in range(count - hop)]
        back = [(order[p + hop], order[p]) for p in range(count - hop)]
        above.insert(0, lax.ppermute(tail[:, rows - size :], "slab", forth))
        below.append(lax.ppermute(head[:, :size], "slab", back))
        need, hop = need - size, hop + 1
    if len(above) == 1:
        return above[0], below[0]
    return jnp.concatenate(above, axis=1), jnp.concatenate(below, axis=1)


def body(estimate, recorded, lateral, axial_taps):
    count = lax.axis_size("slab")
    run = max(count // 4, 1)
    depth, rows, width = estimate.shape[0], estimate.shape[1] // count, estimate.shape[2]
    views, margin = recorded.shape[0], lateral.shape[2] // 2
    last = views - 1
    every = tuple(range(rows))

    current = to_pencils(estimate, count, run, every)
    data = to_pencils(recorded[0], count, run, every)
    blocks, _, planes, _ = current.shape

    def volume(size):
        return jax.ShapeDtypeStruct((blocks, size, planes, width), jnp.float32)

    def held(size):
        return pltpu.VMEM((blocks, size, planes, width), jnp.float32)

    extent, double = padded(rows + 2 * margin), 2 * margin
    end = volume(min(double, rows))
    taps = [normalized(lateral[v, 0]) for v in range(views)]
    columns = [banded(normalized(lateral[v, 1]), width) for v in range(views)]
    depths = [banded(normalized(axial_taps[v]), blocks * planes) for v in range(views)]
    blur_x = [x_matrix(t[::-1], [(-margin, extent)], (0, rows)) for t in taps]
    sides = [(-double, double), (0, rows), (rows, double)]
    spread_x = [x_matrix(t, sides, (-margin, rows + double)) for t in taps[:last]]
    sides = [(-margin, margin), (0, rows), (rows, margin)]
    finish_x = x_matrix(taps[last], sides, (0, rows))

    def matrices(v):
        return blur_x[v], columns[v], depths[v].T, columns[v].T, depths[v]

    outer = 9 * rows // 32
    split = outer >= margin + 1 and outer % 2 == 0 and views > 1
    ends = tuple(r for r in every if r < outer or r >= rows - outer)
    inside = tuple(r for r in every if outer <= r < rows - outer)

    above, below = halos(current[:, :margin], current[:, rows - margin :] if rows > margin else current, margin, count, run)
    for v in range(views):
        if v < last:
            chosen = ends if split and v + 1 == last else every
            order = (head,) if v else ()
            coming = to_pencils(recorded[v + 1], count, run, chosen, order, (above, below))
        if v == 0:
            wide, center, head, tail = call(
                first_kernel, "first", 26, (volume(extent), volume(rows), end, end), [WHOLE] * 9,
                [held(extent), held(rows)],
            )(*matrices(v), above, current, below, data)
        elif v == last and split:
            coming = to_pencils(recorded[v], count, run, inside, (head,), (above, below))
            outs = [volume(n) for n in (rows, rows - 2 * outer, outer, outer, margin, margin)]
            own, blurred, first, second, head, tail = call(
                functools.partial(last_kernel, margin), "last", 30, tuple(outs), [WHOLE] * 11,
                [held(extent), held(extent), held(rows)],
            )(spread_x[v - 1], *matrices(v), above, center, below, wide, data)
        else:
            wide, center, head, tail = call(
                view_kernel, "view", 33, (volume(extent), volume(rows), end, end), [WHOLE] * 11,
                [held(extent), held(rows)],
            )(spread_x[v - 1], *matrices(v), above, center, below, wide, data)
        reach = double
        if v == last:
            reach = margin
            head, tail = head[:, :margin], tail[:, max(tail.shape[1] - margin, 0) :]
        above, below = halos(head, tail, reach, count, run)
        data = coming
    if split:
        inner = call(middle_kernel, "middle", 3, volume(rows - 2 * outer), [WHOLE] * 4)(
            columns[last].T, depths[last], blurred, data
        )
        pieces = [first, inner, second]
    else:
        own, pieces = wide[:, margin : margin + rows], [center]
    step = 4 if blocks % 4 == 0 else 1
    cut = lambda place: (pl.ds(place * step, step),)
    (current,) = streamed(
        functools.partial(finish_part, step),
        "finish",
        7,
        blocks // step,
        [finish_x],
        [above, below, own, *pieces],
        [volume(rows)],
        (cut, cut),
    )
    return to_planes(current, count, run, depth)


def solution(mesh):
    in_specs = (P("slab", "groups", None), P(None, "slab", "groups", None), P(), P())
    out_specs = P("slab", "groups", None)
    return jax.shard_map(body, mesh=mesh, in_specs=in_specs, out_specs=out_specs, check_vma=False)
```

```python
import functools

import jax
import jax.numpy as jnp
import numpy as np
from jax import lax
from jax.experimental import pallas as pl
from jax.experimental.pallas import tpu as pltpu
from jax.sharding import PartitionSpec as P

VMEM_LIMIT = 56 * 1024 * 1024
WHOLE = pl.BlockSpec(memory_space=pltpu.VMEM)
ANYWHERE = pl.BlockSpec(memory_space=pl.ANY)
TURN_US = 4


def cost(microseconds):
    return pl.CostEstimate(flops=0, bytes_accessed=int(microseconds * 3.6e6), transcendentals=0)


def banded(kernel, extent):
    length = kernel.shape[0]
    margin = length // 2
    places = jnp.arange(extent, dtype=jnp.int32)
    offsets = places[None, :] - places[:, None] + margin
    stencil = jnp.arange(length, dtype=jnp.int32)
    picked = (offsets[None, :, :] == stencil[:, None, None]).astype(jnp.float32)
    return jnp.sum(kernel[:, None, None] * picked, axis=0)


def normalized(kernel):
    return kernel / jnp.sum(kernel)


def halves(value):
    high = value.astype(jnp.bfloat16)
    low = (value - high.astype(jnp.float32)).astype(jnp.bfloat16)
    return high, low


def position(device, run):
    row, place = device // run, device % run
    return row * run + jnp.where(row % 2 == 0, place, run - 1 - place)


def device_order(count, run):
    return [r * run + (p if r % 2 == 0 else run - 1 - p) for r in range(count // run) for p in range(run)]


def along_yz(load, store, matrix_y, matrix_z, rows):
    depth, width = matrix_z.shape[0], matrix_y.shape[0]
    right_high, right_low = halves(matrix_y)
    right = jnp.concatenate([right_high, right_low], axis=1)
    right = jnp.concatenate([right, right], axis=0)
    left_high, left_low = halves(matrix_z)
    left = jnp.concatenate([left_high, left_low], axis=0)
    left = jnp.concatenate([left, left], axis=1)

    def pair(index, _):
        row = 2 * index
        planes = jnp.concatenate([load(row), load(row + 1)], axis=0)
        product = jnp.dot(
            jnp.concatenate(halves(planes), axis=1), right, preferred_element_type=jnp.float32
        )
        mixed = product[:, :width] + product[:, width:]
        sides = jnp.concatenate([mixed[:depth], mixed[depth:]], axis=1)
        product = jnp.dot(
            left, jnp.concatenate(halves(sides), axis=0), preferred_element_type=jnp.float32
        )
        mixed = product[:depth] + product[depth:]
        store(row, mixed[:, :width])
        store(row + 1, mixed[:, width:])
        return 0

    lax.fori_loop(0, rows // 2, pair, 0, unroll=4)


def x_plane(ref, block, plane):
    blocks, rows, planes, width = ref.shape
    flat = ref.reshape(blocks * rows * planes, width)
    return flat[pl.ds(block * rows * planes + plane, rows, stride=planes), :]


def set_x_plane(ref, block, plane, value):
    blocks, rows, planes, width = ref.shape
    flat = ref.reshape(blocks * rows * planes, width)
    flat[pl.ds(block * rows * planes + plane, rows, stride=planes), :] = value


def padded(size):
    return -(-size // 16) * 16


def along_x(groups, matrix, emit, first=0, blocks=None):
    _, _, planes, width = groups[0][0].shape
    blocks = groups[0][0].shape[0] if blocks is None else blocks
    left_high, left_low = halves(matrix)
    left = jnp.concatenate([left_high, left_low], axis=0)
    left = jnp.concatenate([left, left], axis=1)

    def column(block, plane):
        parts = []
        for group in groups:
            parts += [x_plane(piece, block, plane) for piece in group]
            size = sum(piece.shape[1] for piece in group)
            if padded(size) > size:
                parts.append(jnp.zeros((padded(size) - size, width), jnp.float32))
        return jnp.concatenate(parts, axis=0)

    def pair(index, _):
        block, plane = first + index // (planes // 2), (index % (planes // 2)) * 2
        columns = jnp.concatenate([column(block, plane), column(block, plane + 1)], axis=1)
        product = jnp.dot(
            left, jnp.concatenate(halves(columns), axis=0), preferred_element_type=jnp.float32
        )
        mixed = product[: product.shape[0] // 2] + product[product.shape[0] // 2 :]
        emit(block, plane, mixed[:, :width])
        emit(block, plane + 1, mixed[:, width:])
        return 0

    lax.fori_loop(0, blocks * planes // 2, pair, 0, unroll=8)


def x_matrix(taps, groups, target):
    margin, nowhere = taps.shape[0] // 2, 1 << 20
    source = np.concatenate(
        [np.r_[np.arange(x, x + n), np.full(padded(n) - n, nowhere)] for x, n in groups]
    )
    rows = np.arange(padded(target[1]))
    offset = source[None, :] - (target[0] + rows)[:, None] + margin
    offset = np.where(rows[:, None] < target[1], offset, -1).astype(np.int32)
    stencil = jnp.arange(taps.shape[0], dtype=jnp.int32)
    picked = (jnp.asarray(offset)[None] == stencil[:, None, None]).astype(jnp.float32)
    return jnp.sum(taps[:, None, None] * picked, axis=0)


def plane_loader(ref):
    blocks, _, planes, width = ref.shape
    return lambda row: ref[:, row].reshape(blocks * planes, width)


def plane_storer(ref):
    blocks, _, planes, width = ref.shape

    def store(row, value):
        ref[:, row] = value.reshape(blocks, planes, width)

    return store


def copy_ends(first, second, head, tail):
    rows, kept = second.shape[1], head.shape[1]
    head[...] = first[:, :kept]
    tail[...] = second[:, rows - kept :]


def divide_yz(blurred, data, out, matrix_y, matrix_z, begin=0, place=0):
    data_of, blurred_of = plane_loader(data), plane_loader(blurred)
    along_yz(
        lambda row: data_of(place + row) / blurred_of(begin + row),
        plane_storer(out),
        matrix_y,
        matrix_z,
        out.shape[1],
    )


def blur(wide, mixed, blurred, blur_x, blur_y, blur_z):
    along_yz(plane_loader(wide), plane_storer(mixed), blur_y[...], blur_z[...], wide.shape[1])
    rows = blurred.shape[1]
    along_x([[mixed]], blur_x[...], lambda b, p, value: set_x_plane(blurred, b, p, value[:rows]))


def update(spread_x, above, center, below, before, wide):
    rows = wide.shape[1]

    def emit(block, plane, value):
        set_x_plane(wide, block, plane, x_plane(before, block, plane) * value[:rows])

    along_x([[above], [center], [below]], spread_x[...], emit)


def first_kernel(
    blur_x, blur_y, blur_z, back_y, back_z, above, own, below, data, wide, out, head, tail, mixed, blurred
):
    margin, rows = above.shape[1], own.shape[1]
    wide[:, :margin] = above[...]
    wide[:, margin : margin + rows] = own[...]
    wide[:, margin + rows : rows + 2 * margin] = below[...]
    if wide.shape[1] > rows + 2 * margin:
        wide[:, rows + 2 * margin :] = jnp.zeros_like(wide[:, rows + 2 * margin :])
    blur(wide, mixed, blurred, blur_x, blur_y, blur_z)
    divide_yz(blurred, data, out, back_y[...], back_z[...])
    copy_ends(out, out, head, tail)


def view_kernel(
    spread_x, blur_x, blur_y, blur_z, back_y, back_z, above, center, below, before, data,
    wide, out, head, tail, mixed, blurred,
):
    update(spread_x, above, center, below, before, wide)
    blur(wide, mixed, blurred, blur_x, blur_y, blur_z)
    divide_yz(blurred, data, out, back_y[...], back_z[...])
    copy_ends(out, out, head, tail)


def last_kernel(
    margin, spread_x, blur_x, blur_y, blur_z, back_y, back_z, above, center, below, before, data,
    own, inner, out_0, out_1, head, tail, wide, mixed, blurred,
):
    update(spread_x, above, center, below, before, wide)
    own[...] = wide[:, margin : margin + own.shape[1]]
    blur(wide, mixed, blurred, blur_x, blur_y, blur_z)
    outer, between = out_0.shape[1], inner.shape[1]
    inner[...] = blurred[:, outer : outer + between]
    divide_yz(blurred, data, out_0, back_y[...], back_z[...])
    divide_yz(blurred, data, out_1, back_y[...], back_z[...], outer + between, outer)
    copy_ends(out_0, out_1, head, tail)


def middle_kernel(back_y, back_z, blurred, data, out):
    divide_yz(blurred, data, out, back_y[...], back_z[...])


def finish_part(blocks, step, fixed, sources, targets):
    (spread_x,), (above, below, current, *pieces), (updated,) = fixed, sources, targets
    rows = updated.shape[1]

    def emit(block, plane, value):
        set_x_plane(updated, block, plane, x_plane(current, block, plane) * value[:rows])

    along_x([[above], pieces, [below]], spread_x[...], emit, step * blocks, blocks)


def streamed(part, name, microseconds, steps, fixed, inputs, outs, cuts, after=(), spare=0):
    counts = len(fixed), len(inputs), len(after), len(outs), len(inputs), len(outs)

    def kernel(*refs):
        groups, start = [], 0
        for size in counts:
            groups.append(refs[start : start + size])
            start += size
        held, sources, _, targets, ins, ready = groups
        in_sem, out_sem = refs[start:]

        def come(k, step):
            cut = cuts[0](step)
            return pltpu.make_async_copy(sources[k].at[cut], ins[k].at[cut], in_sem.at[k, step])

        def go(k, step):
            cut = cuts[1](step)
            return pltpu.make_async_copy(ready[k].at[cut], targets[k].at[cut], out_sem.at[k, step])

        def begin(step, _):
            for k in range(len(inputs)):
                come(k, step).start()
            return 0

        def work(step, _):
            for k in range(len(inputs)):
                come(k, step).wait()
            part(step, held, ins, ready)
            for k in range(len(outs)):
                go(k, step).start()
            return 0

        def end(step, _):
            for k in range(len(outs)):
                go(k, step).wait()
            return 0

        lax.fori_loop(0, steps, begin, 0)
        lax.fori_loop(0, steps, work, 0)
        lax.fori_loop(0, steps, end, 0)

    def scratch(array, more):
        shape = array.shape if len(array.shape) == 4 else (array.shape[0], array.shape[1] + more, array.shape[2])
        return pltpu.VMEM(shape, jnp.float32)

    return pl.pallas_call(
        kernel,
        out_shape=outs,
        in_specs=[WHOLE] * len(fixed) + [ANYWHERE] * (len(inputs) + len(after)),
        out_specs=[ANYWHERE] * len(outs),
        scratch_shapes=[scratch(array, spare) for array in inputs]
        + [scratch(array, 0) for array in outs]
        + [pltpu.SemaphoreType.DMA((len(inputs), steps)), pltpu.SemaphoreType.DMA((len(outs), steps))],
        compiler_params=pltpu.CompilerParams(vmem_limit_bytes=VMEM_LIMIT),
        cost_estimate=cost(microseconds),
        name=name,
    )(*fixed, *inputs, *after)


def call(kernel, name, microseconds, outs, in_specs, scratch=()):
    return pl.pallas_call(
        kernel,
        out_shape=outs,
        in_specs=in_specs,
        out_specs=jax.tree.map(lambda _: WHOLE, outs),
        scratch_shapes=list(scratch),
        compiler_params=pltpu.CompilerParams(vmem_limit_bytes=VMEM_LIMIT),
        cost_estimate=cost(microseconds),
        name=name,
    )


def x_rows(device, run, rows):
    return pl.ds(pl.multiple_of(position(device, run) * rows, 8), rows)


def turn_part(run, rows, chosen, device, _, sources, targets):
    (source,), (target,) = sources, targets
    depth, extent, width = source.shape
    flat = source.reshape(depth * extent, width)
    base = position(device, run) * rows
    for place, row in enumerate(chosen):
        target[device, place] = flat[pl.ds(base + row, depth, stride=extent), :]


def turn_back_part(run, device, _, sources, targets):
    (source,), (target,) = sources, targets
    count, rows, depth, width = source.shape
    flat = source.reshape(count * rows * depth, width)
    base = position(device, run) * rows
    for plane in range(depth):
        for row in range(0, rows, 8):
            target[plane, pl.ds(pl.multiple_of(base + row, 8), 8), :] = flat[
                pl.ds((device * rows + row) * depth + plane, 8, stride=depth), :
            ]


def gate(blocks, arrays):
    return pl.pallas_call(
        lambda *refs: None,
        out_shape=jax.ShapeDtypeStruct(blocks.shape, blocks.dtype),
        in_specs=[ANYWHERE] * (1 + len(arrays)),
        out_specs=ANYWHERE,
        input_output_aliases={0: 0},
        cost_estimate=cost(0.5),
        name="gate",
    )(blocks, *arrays)


def to_pencils(planes, count, run, chosen, turn_after=(), send_after=()):
    depth, extent, width = planes.shape
    rows = extent // count
    size = len(chosen)
    if depth % 8 == 0 and rows % 8 == 0:
        (blocks,) = streamed(
            functools.partial(turn_part, run, rows, chosen),
            "turn",
            TURN_US,
            count,
            [],
            [planes],
            [jax.ShapeDtypeStruct((count, size, depth, width), planes.dtype)],
            (lambda step: (slice(None), x_rows(step, run, rows)), lambda step: (pl.ds(step, 1),)),
            turn_after,
            8,
        )
        if send_after:
            blocks = gate(blocks, send_after)
        return lax.all_to_all(blocks, "slab", split_axis=0, concat_axis=0, tiled=True)
    order = device_order(count, run)
    blocks = planes.reshape(depth, count, rows, width)[:, :, np.array(chosen)].transpose(1, 0, 2, 3)
    blocks = jnp.stack([blocks[order.index(d)] for d in range(count)])
    blocks = lax.all_to_all(blocks, "slab", split_axis=0, concat_axis=0, tiled=True)
    return blocks.reshape(1, count * depth, size, width).swapaxes(1, 2)


def to_planes(pencils, count, run, depth):
    rows, width = pencils.shape[1], pencils.shape[3]
    if depth % 8 == 0 and rows % 8 == 0:
        blocks = lax.all_to_all(pencils, "slab", split_axis=0, concat_axis=0, tiled=True)
        return streamed(
            functools.partial(turn_back_part, run),
            "turn_back",
            TURN_US,
            count,
            [],
            [blocks],
            [jax.ShapeDtypeStruct((depth, rows * count, width), pencils.dtype)],
            (lambda step: (pl.ds(step, 1),), lambda step: (slice(None), x_rows(step, run, rows))),
        )[0]
    order = device_order(count, run)
    blocks = pencils.swapaxes(1, 2).reshape(count, depth, rows, width)
    blocks = lax.all_to_all(blocks, "slab", split_axis=0, concat_axis=0, tiled=True)
    blocks = jnp.stack([blocks[d] for d in order])
    return blocks.transpose(1, 0, 2, 3).reshape(depth, rows * count, width)


def halos(head, tail, margin, count, run):
    order = device_order(count, run)
    rows = head.shape[1]
    above, below, need, hop = [], [], margin, 1
    while need > 0:
        size = min(rows, need)
        forth = [(order[p], order[p + hop]) for p in range(count - hop)]
        back = [(order[p + hop], order[p]) for p in range(count - hop)]
        above.insert(0, lax.ppermute(tail[:, rows - size :], "slab", forth))
        below.append(lax.ppermute(head[:, :size], "slab", back))
        need, hop = need - size, hop + 1
    if len(above) == 1:
        return above[0], below[0]
    return jnp.concatenate(above, axis=1), jnp.concatenate(below, axis=1)


def body(estimate, recorded, lateral, axial_taps):
    count = lax.axis_size("slab")
    run = max(count // 4, 1)
    depth, rows, width = estimate.shape[0], estimate.shape[1] // count, estimate.shape[2]
    views, margin = recorded.shape[0], lateral.shape[2] // 2
    last = views - 1
    every = tuple(range(rows))

    current = to_pencils(estimate, count, run, every)
    data = to_pencils(recorded[0], count, run, every)
    blocks, _, planes, _ = current.shape

    def volume(size):
        return jax.ShapeDtypeStruct((blocks, size, planes, width), jnp.float32)

    def held(size):
        return pltpu.VMEM((blocks, size, planes, width), jnp.float32)

    extent, double = padded(rows + 2 * margin), 2 * margin
    end = volume(min(double, rows))
    taps = [normalized(lateral[v, 0]) for v in range(views)]
    columns = [banded(normalized(lateral[v, 1]), width) for v in range(views)]
    depths = [banded(normalized(axial_taps[v]), blocks * planes) for v in range(views)]
    blur_x = [x_matrix(t[::-1], [(-margin, extent)], (0, rows)) for t in taps]
    sides = [(-double, double), (0, rows), (rows, double)]
    spread_x = [x_matrix(t, sides, (-margin, rows + double)) for t in taps[:last]]
    sides = [(-margin, margin), (0, rows), (rows, margin)]
    finish_x = x_matrix(taps[last], sides, (0, rows))

    def matrices(v):
        return blur_x[v], columns[v], depths[v].T, columns[v].T, depths[v]

    outer = rows // 4
    split = outer >= margin + 1 and outer % 2 == 0 and views > 1
    ends = tuple(r for r in every if r < outer or r >= rows - outer)
    inside = tuple(r for r in every if outer <= r < rows - outer)

    above, below = halos(current[:, :margin], current[:, rows - margin :] if rows > margin else current, margin, count, run)
    for v in range(views):
        if v < last:
            chosen = ends if split and v + 1 == last else every
            order = (head,) if v else ()
            coming = to_pencils(recorded[v + 1], count, run, chosen, order, (above, below))
        if v == 0:
            wide, center, head, tail = call(
                first_kernel, "first", 26, (volume(extent), volume(rows), end, end), [WHOLE] * 9,
                [held(extent), held(rows)],
            )(*matrices(v), above, current, below, data)
        elif v == last and split:
            coming = to_pencils(recorded[v], count, run, inside, (head,), (above, below))
            outs = [volume(n) for n in (rows, rows - 2 * outer, outer, outer, margin, margin)]
            own, blurred, first, second, head, tail = call(
                functools.partial(last_kernel, margin), "last", 30, tuple(outs), [WHOLE] * 11,
                [held(extent), held(extent), held(rows)],
            )(spread_x[v - 1], *matrices(v), above, center, below, wide, data)
        else:
            wide, center, head, tail = call(
                view_kernel, "view", 33, (volume(extent), volume(rows), end, end), [WHOLE] * 11,
                [held(extent), held(rows)],
            )(spread_x[v - 1], *matrices(v), above, center, below, wide, data)
        reach = double
        if v == last:
            reach = margin
            head, tail = head[:, :margin], tail[:, max(tail.shape[1] - margin, 0) :]
        above, below = halos(head, tail, reach, count, run)
        data = coming
    if split:
        inner = call(middle_kernel, "middle", 3, volume(rows - 2 * outer), [WHOLE] * 4)(
            columns[last].T, depths[last], blurred, data
        )
        pieces = [first, inner, second]
    else:
        own, pieces = wide[:, margin : margin + rows], [center]
    step = 4 if blocks % 4 == 0 else 1
    cut = lambda place: (pl.ds(place * step, step),)
    (current,) = streamed(
        functools.partial(finish_part, step),
        "finish",
        7,
        blocks // step,
        [finish_x],
        [above, below, own, *pieces],
        [volume(rows)],
        (cut, cut),
    )
    return to_planes(current, count, run, depth)


def solution(mesh):
    in_specs = (P("slab", "groups", None), P(None, "slab", "groups", None), P(), P())
    out_specs = P("slab", "groups", None)
    return jax.shard_map(body, mesh=mesh, in_specs=in_specs, out_specs=out_specs, check_vma=False)
```
